256 devices in a mesh: dp: 4 (over y_hi, core), seq: 64 (over x, y_lo, z).
Axes of the slice: x: 4, y: 4 (y_hi: 2, y_lo: 2; y = y_hi * 2 + y_lo), z: 8, core: 2. Of those that a mesh axis runs over, the one named last changes fastest.
Arguments:
- q_raw: bfloat16 [4, 8192, 1536], P('dp', 'seq'), may hold values from -6 to 6
- k_raw: bfloat16 [4, 8192, 1536], P('dp', 'seq'), may hold values from -6 to 6
- values: bfloat16 [4, 8192, 1536], P('dp', 'seq'), may hold values from -6 to 6
- d_out: bfloat16 [4, 8192, 1536], P('dp', 'seq'), may hold values from -14 to 14
- q_gain: float32 [128], replicated, may hold values from 1 to 2.5
- k_gain: float32 [128], replicated, may hold values from 1 to 2.5
Outputs:
- q_grad: bfloat16 [4, 8192, 1536], P('dp', 'seq')
- k_grad: bfloat16 [4, 8192, 1536], P('dp', 'seq')
- v_grad: bfloat16 [4, 8192, 1536], P('dp', 'seq')
- q_gain_grad: float32 [128], replicated
- k_gain_grad: float32 [128], replicated
The draws below stay inside these ranges and needn't reach their ends.
All inputs are finite; a program needn't handle non-finite values.
Results may differ from the reference program's by a relative error of at most 0.012.
The reference program's roundings to bfloat16 on the way count: a program that leaves them out, or rounds other values in their place, can miss the bound.
Values may be sent and summed in bfloat16 or wider, within the bound.
No kernel may reach another device: no remote copies, remote signals or barrier semaphores. Data moves between devices by JAX's collectives and lax.ppermute only.
A program may use at most 256 MiB of HBM per device.

```python
import math
import jax
import jax.numpy as jnp
from jax import lax

HEADS = 12
HD = 128
TILE_TOK = 64
BF = 1
BH = 1
BW = 2
DEV_H = 2
DEV_W = 4
DEV_F = 8
VIDEOS = 4
TOKENS = 8192


def draw_d_out(key, part):
    key = jax.random.fold_in(key, 7)
    first_key, second_key = jax.random.split(key)
    tile_count = VIDEOS * TOKENS // TILE_TOK
    entries = jnp.clip(jax.random.normal(first_key, (tile_count, TILE_TOK, HEADS * HD), jnp.float32), -4.0, 4.0)
    scales = jnp.exp(jax.random.uniform(second_key, (tile_count, 1, 1), jnp.float32, -1.2, 1.2))
    return (entries * scales).reshape(VIDEOS, TOKENS, HEADS * HD).astype(jnp.bfloat16)


def block_scale(stream_key, extent, shards, smallest, top_value):
    def one(position, blocks):
        heights = jax.random.uniform(jax.random.fold_in(jax.random.fold_in(stream_key, 6), position), (blocks,), jnp.float32, smallest / len(shards), top_value / len(shards))
        return jnp.repeat(jnp.exp(heights), extent[position] // blocks).reshape((-1,) + (1,) * (len(extent) - position - 1))

    gain = one(*shards[0])
    for cut in shards[1:]:
        gain = gain * one(*cut)
    return gain


def scatter_about(rng, extent, scale, most, pieces=(), dtype=jnp.bfloat16):
    values = scale * jax.random.normal(rng, extent, jnp.float32)
    if pieces:
        values = values * block_scale(rng, extent, pieces, -0.22, 0.18)
    return jnp.clip(values, -most, most).astype(dtype)


def setup_inputs(seed: int = 0) -> dict:
    splits = jax.random.split(jax.random.key(seed), 7)
    q_raw = scatter_about(splits[0], (VIDEOS, TOKENS, HEADS * HD), 1.0, 6.0, ((0, 4), (1, 64)))
    k_raw = scatter_about(splits[1], (VIDEOS, TOKENS, HEADS * HD), 1.0, 6.0, ((0, 4), (1, 64)))
    values = scatter_about(splits[2], (VIDEOS, TOKENS, HEADS * HD), 1.0, 6.0, ((0, 4), (1, 64)))
    d_out = draw_d_out(jax.random.fold_in(splits[6], 71), 0)
    q_gain = jnp.clip(jnp.exp(jax.random.uniform(splits[4], (HD,), jnp.float32, math.log(1.0), math.log(2.5))), 1.0, 2.5)
    k_gain = jnp.clip(jnp.exp(jax.random.uniform(splits[5], (HD,), jnp.float32, math.log(1.0), math.log(2.5))), 1.0, 2.5)
    return dict(q_raw=q_raw, k_raw=k_raw, values=values, d_out=d_out, q_gain=q_gain, k_gain=k_gain)


EPSILON = 1e-06

def product(form, left, right):
    return jnp.einsum(form, left.astype(jnp.float32), right.astype(jnp.float32), precision=lax.Precision.HIGHEST)

def normalize(source, scaling):
    inputs = source.astype(jnp.float32)
    inverse = lax.rsqrt(lax.optimization_barrier(jnp.mean(inputs * inputs, axis=-1, keepdims=True)) + EPSILON)
    return (inputs, inverse, inputs * inverse * scaling)

def norm_back(inputs, inverse, scaling, cotangent):
    scaled = cotangent * scaling
    input_grad = inverse * scaled - inputs * inverse * inverse * inverse * lax.optimization_barrier(jnp.mean(inputs * scaled, axis=-1, keepdims=True))
    gain_grad = lax.optimization_barrier(jnp.sum((cotangent * inputs * inverse).reshape(-1, inputs.shape[-1]), axis=0))
    return (input_grad, gain_grad)

def offsets():
    return [(a, b, c) for a in (-1, 0, 1) for b in (-1, 0, 1) for c in (-1, 0, 1)]

def window(extended, a, b, c, grid_dims):
    return extended[1 + a:1 + a + grid_dims[0], 1 + b:1 + b + grid_dims[1], 1 + c:1 + c + grid_dims[2]]

def tile_mask(inside, a, b, c, grid_dims):
    along_f = inside[0][1 + a:1 + a + grid_dims[0]]
    along_h = inside[1][1 + b:1 + b + grid_dims[1]]
    along_w = inside[2][1 + c:1 + c + grid_dims[2]]
    keep = along_f[:, None, None] & along_h[None, :, None] & along_w[None, None, :]
    return keep.reshape(-1, 1, 1, 1)

def attend(q_tiles, key_ext, value_ext, inside, grid_dims):
    tile_shape = q_tiles.shape
    scale = tile_shape[-1] ** (-0.5)
    logit_list = []
    normalizer = jnp.zeros((tile_shape[0], tile_shape[2], tile_shape[1]), jnp.float32)
    for a, b, c in offsets():
        key_tile = window(key_ext, a, b, c, grid_dims).reshape(tile_shape)
        logits = product('tqhd,tkhd->thqk', q_tiles, key_tile) * scale
        keep = tile_mask(inside, a, b, c, grid_dims)
        logit_list.append((logits, keep))
        normalizer = normalizer + lax.optimization_barrier(jnp.sum(jnp.where(keep, jnp.exp(logits), 0.0), axis=-1))
    log_norm = jnp.log(normalizer)
    chances = []
    attended = jnp.zeros(tile_shape, jnp.float32)
    for number, (a, b, c) in enumerate(offsets()):
        logits, keep = logit_list[number]
        chance = jnp.where(keep, jnp.exp(logits - log_norm[..., None]), 0.0)
        chances.append(chance)
        value_tile = window(value_ext, a, b, c, grid_dims).reshape(tile_shape)
        attended = attended + product('thqk,tkhd->tqhd', chance.astype(jnp.bfloat16), value_tile)
    return (chances, log_norm, attended)

def backward(q_tiles, key_ext, value_ext, upstream, chances, row_dot, grid_dims):
    tile_shape = q_tiles.shape
    dot_rows = jnp.transpose(row_dot, (0, 2, 1))[..., None]
    query_grad = jnp.zeros(tile_shape, jnp.float32)
    key_ext_grad = jnp.zeros(key_ext.shape, jnp.float32)
    value_ext_grad = jnp.zeros(key_ext.shape, jnp.float32)
    for number, (a, b, c) in enumerate(offsets()):
        chance = chances[number]
        key_tile = window(key_ext, a, b, c, grid_dims).reshape(tile_shape)
        value_tile = window(value_ext, a, b, c, grid_dims).reshape(tile_shape)
        weight_grad = product('tqhd,tkhd->thqk', upstream, value_tile)
        score_grad = (chance * (weight_grad - dot_rows)).astype(jnp.bfloat16)
        query_grad = query_grad + product('thqk,tkhd->tqhd', score_grad, key_tile)
        region = (slice(1 + a, 1 + a + grid_dims[0]), slice(1 + b, 1 + b + grid_dims[1]), slice(1 + c, 1 + c + grid_dims[2]))
        key_ext_grad = key_ext_grad.at[region].add(product('thqk,tqhd->tkhd', score_grad, q_tiles).reshape(grid_dims + tile_shape[1:]))
        value_ext_grad = value_ext_grad.at[region].add(product('thqk,tqhd->tkhd', chance.astype(jnp.bfloat16), upstream).reshape(grid_dims + tile_shape[1:]))
    return (query_grad, key_ext_grad, value_ext_grad)

def to_grid(source):
    moved = source.reshape(DEV_F, DEV_H, DEV_W, BF, BH, BW, TILE_TOK, HEADS, HD)
    moved = moved.transpose(0, 3, 1, 4, 2, 5, 6, 7, 8)
    return moved.reshape(DEV_F * BF, DEV_H * BH, DEV_W * BW, TILE_TOK, HEADS, HD)

def from_grid(source):
    moved = source.reshape(DEV_F, BF, DEV_H, BH, DEV_W, BW, TILE_TOK, HEADS * HD)
    return moved.transpose(0, 2, 4, 1, 3, 5, 6, 7).reshape(TOKENS, HEADS * HD)

def one_video(q_video, k_video, v_video, cotangent, q_gain, k_gain):
    grid_dims = (DEV_F * BF, DEV_H * BH, DEV_W * BW)
    q_source, q_inverse, q_normed = normalize(to_grid(q_video), q_gain)
    k_source, k_inverse, k_normed = normalize(to_grid(k_video), k_gain)
    q_tiles = q_normed.astype(jnp.bfloat16).reshape(-1, TILE_TOK, HEADS, HD)
    padding = ((1, 1), (1, 1), (1, 1), (0, 0), (0, 0), (0, 0))
    key_ext = jnp.pad(k_normed.astype(jnp.bfloat16), padding)
    value_ext = jnp.pad(to_grid(v_video), padding)
    inside = tuple(((jnp.arange(n + 2) >= 1) & (jnp.arange(n + 2) <= n) for n in grid_dims))
    chances, log_norm, attended = attend(q_tiles, key_ext, value_ext, inside, grid_dims)
    upstream = to_grid(cotangent).reshape(q_tiles.shape)
    row_dot = lax.optimization_barrier(jnp.sum(upstream.astype(jnp.float32) * attended, axis=-1))
    query_grad, key_ext_grad, value_ext_grad = backward(q_tiles, key_ext, value_ext, upstream, chances, row_dot, grid_dims)
    scale = HD ** (-0.5)
    query_grad = (scale * query_grad).reshape(q_source.shape)
    key_grad = scale * key_ext_grad[1:-1, 1:-1, 1:-1]
    value_grad = value_ext_grad[1:-1, 1:-1, 1:-1]
    q_input_grad, q_gain_part = norm_back(q_source, q_inverse, q_gain, query_grad)
    k_input_grad, k_gain_part = norm_back(k_source, k_inverse, k_gain, key_grad)
    return (from_grid(q_input_grad).astype(jnp.bfloat16), from_grid(k_input_grad).astype(jnp.bfloat16), from_grid(value_grad).astype(jnp.bfloat16), q_gain_part, k_gain_part)

def reference(q_raw, k_raw, values, d_out, q_gain, k_gain):
    q_grad, k_grad, v_grad, q_parts, k_parts = lax.map(lambda arrays: one_video(arrays[0], arrays[1], arrays[2], arrays[3], q_gain, k_gain), (q_raw, k_raw, values, d_out))
    return (q_grad, k_grad, v_grad, lax.optimization_barrier(jnp.sum(q_parts, axis=0)), lax.optimization_barrier(jnp.sum(k_parts, axis=0)))
```

```python
import functools

import jax
import jax.numpy as jnp
from jax import lax
from jax.experimental import pallas as pl
from jax.experimental.pallas import tpu as pltpu
from jax.sharding import Mesh
from jax.sharding import PartitionSpec as P

HEADS = 12
HD = 128
TILE = 64
PAIR = 2 * TILE
GROUP = 16
HALF = 8
COLS = 4
WIDE = 8
EXTRA = 16
EPSILON = 1e-06
SCALE = HD ** (-0.5)
SCALE_LOG2E = SCALE * 1.4426950408889634
F32 = jnp.float32
BF16 = jnp.bfloat16
VMEM_BYTES = 48 * 1024 * 1024

SLAB = 2 * TILE
COLUMN = 4 * SLAB
PARTS = ((0, SLAB, 0, SLAB), (SLAB, 2 * SLAB, 0, 2 * SLAB), (3 * SLAB, SLAB, SLAB, SLAB))


def nt(left, right):
    return lax.dot_general(left, right, (((1,), (1,)), ((), ())), preferred_element_type=F32)


def nn(left, right):
    return lax.dot_general(left, right, (((1,), (0,)), ((), ())), preferred_element_type=F32)


def inverse_rms(inputs):
    return lax.rsqrt(jnp.mean(inputs * inputs, axis=-1, keepdims=True) + EPSILON)


def norm_back(inputs, inverse, gain, cotangent):
    scaled = cotangent * gain
    mean = jnp.mean(inputs * scaled, axis=-1, keepdims=True)
    return inverse * scaled - inputs * (inverse * inverse * inverse * mean)


def pack_kernel(first_ref, second_ref, out_ref):
    for head in range(HEADS):
        lanes = slice(head * HD, (head + 1) * HD)
        out_ref[head, 0] = first_ref[0, :, lanes]
        out_ref[head, 1] = second_ref[0, :, lanes]
    for head in range(HEADS, GROUP):
        out_ref[head] = jnp.zeros(out_ref.shape[1:], out_ref.dtype)


def pack(first, second):
    return pl.pallas_call(
        pack_kernel,
        out_shape=jax.ShapeDtypeStruct((GROUP, 2, PAIR, HD), BF16),
        name="pack",
        compiler_params=pltpu.CompilerParams(vmem_limit_bytes=VMEM_BYTES),
    )(first, second)


def attention_kernel(
    flags_ref,
    kv_ref,
    low_ref,
    high_ref,
    qd_ref,
    q_gain_ref,
    k_gain_ref,
    dq_ref,
    own_ref,
    to_low_ref,
    to_high_ref,
    kn,
    knt,
    vv,
    qn,
    dd,
    dk,
    dv,
    gains,
):
    q_gain = q_gain_ref[...]
    k_gain = k_gain_ref[...]

    def key_block(source, index, frame, row, col):
        raw = source[index, 0].astype(F32)
        normed = (raw * inverse_rms(raw) * k_gain).astype(BF16)
        for part in range(2):
            at = (2 * col + part) * COLUMN + frame * SLAB + row * TILE
            kn[at : at + TILE] = normed[part * TILE : (part + 1) * TILE]
            vv[at : at + TILE] = source[index, 1, part * TILE : (part + 1) * TILE]

    for row in range(2):
        for col in range(COLS):
            key_block(low_ref, row * COLS + col, 0, row, col)
            key_block(kv_ref, row * COLS + col, 1, row, col)
            key_block(kv_ref, HALF + row * COLS + col, 2, row, col)
            key_block(high_ref, row * COLS + col, 3, row, col)
    for block in range(WIDE * COLUMN // HD):
        rows = slice(block * HD, (block + 1) * HD)
        knt[:, rows] = kn[rows].T
    for frame in range(2):
        for row in range(2):
            for col in range(COLS):
                index = frame * HALF + row * COLS + col
                raw = qd_ref[index, 0].astype(F32)
                normed = (raw * inverse_rms(raw) * q_gain).astype(BF16)
                for part in range(2):
                    at = (2 * col + part) * 2 * SLAB + frame * SLAB + row * TILE
                    qn[at : at + TILE] = normed[part * TILE : (part + 1) * TILE]
                    dd[at : at + TILE] = qd_ref[index, 1, part * TILE : (part + 1) * TILE]
    dk[...] = jnp.zeros_like(dk)
    dv[...] = jnp.zeros_like(dv)
    gains[...] = jnp.zeros_like(gains)
    low_valid = flags_ref[0].astype(F32)
    high_valid = flags_ref[1].astype(F32)
    valid = (low_valid, None, high_valid)

    def column(w, steps):
        q_rows = pl.ds(pl.multiple_of(w * (2 * SLAB), 2 * SLAB), 2 * SLAB)
        q_tile = qn[q_rows]
        d_tile = dd[q_rows]
        pieces = []
        total = [jnp.zeros((1, SLAB), F32), jnp.zeros((1, SLAB), F32)]
        for step in steps:
            base = (w + step) * COLUMN
            for number, (first, count, q_first, q_count) in enumerate(PARTS):
                rows = pl.ds(pl.multiple_of(base + first, SLAB), count)
                queries = slice(q_first, q_first + q_count)
                weights = jnp.exp2(nt(kn[rows], q_tile[queries]) * SCALE_LOG2E)
                if valid[number] is not None:
                    weights = weights * valid[number]
                sums = jnp.sum(weights, axis=0, keepdims=True)
                for frame in range(2):
                    if q_first <= frame * SLAB < q_first + q_count:
                        at = frame * SLAB - q_first
                        total[frame] = total[frame] + sums[:, at : at + SLAB]
                weight_grad = nt(vv[rows], d_tile[queries])
                pieces.append((rows, queries, weights, weight_grad))
        reciprocal = 1.0 / jnp.concatenate(total, axis=1)
        dots = [jnp.zeros((1, SLAB), F32), jnp.zeros((1, SLAB), F32)]
        chances = []
        for rows, queries, weights, weight_grad in pieces:
            chance = weights * reciprocal[:, queries]
            rounded = chance.astype(BF16)
            sums = jnp.sum(rounded.astype(F32) * weight_grad, axis=0, keepdims=True)
            for frame in range(2):
                if queries.start <= frame * SLAB < queries.stop:
                    at = frame * SLAB - queries.start
                    dots[frame] = dots[frame] + sums[:, at : at + SLAB]
            chances.append(chance)
            dv[rows] += nn(rounded, d_tile[queries])
        row_dot = jnp.concatenate(dots, axis=1)
        query_grad = [jnp.zeros((HD, SLAB), F32), jnp.zeros((HD, SLAB), F32)]
        for (rows, queries, _, weight_grad), chance in zip(pieces, chances):
            score_grad = (chance * (weight_grad - row_dot[:, queries])).astype(BF16)
            dk[rows] += nn(score_grad, q_tile[queries])
            part_grad = nn(knt[:, rows], score_grad)
            for frame in range(2):
                if queries.start <= frame * SLAB < queries.stop:
                    at = frame * SLAB - queries.start
                    query_grad[frame] = query_grad[frame] + part_grad[:, at : at + SLAB]
        col = w // 2
        place = pl.ds(pl.multiple_of((w % 2) * TILE, TILE), TILE)
        for frame in range(2):
            grad = query_grad[frame].T * SCALE
            for row in range(2):
                index = frame * HALF + row * COLS + col
                raw = qd_ref[index, 0, place].astype(F32)
                inverse = inverse_rms(raw)
                part = grad[row * TILE : (row + 1) * TILE]
                gains[0:8] += jnp.sum((part * raw * inverse).reshape(-1, 8, HD), axis=0)
                dq_ref[index, place] = norm_back(raw, inverse, q_gain, part).astype(BF16)

    column(0, (0, 1))

    def middle(w, carry):
        column(w, (-1, 0, 1))
        return carry

    lax.fori_loop(1, WIDE - 1, middle, 0)
    column(WIDE - 1, (-1, 0))

    def finish(source, index, frame, row, col):
        raw = source[index, 0].astype(F32)
        inverse = inverse_rms(raw)
        keys, vals = [], []
        for part in range(2):
            at = (2 * col + part) * COLUMN + frame * SLAB + row * TILE
            keys.append(dk[at : at + TILE])
            vals.append(dv[at : at + TILE])
        key_grad = jnp.concatenate(keys, axis=0) * SCALE
        gains[8:16] += jnp.sum((key_grad * raw * inverse).reshape(-1, 8, HD), axis=0)
        return key_grad, jnp.concatenate(vals, axis=0)

    for row in range(2):
        for col in range(COLS):
            index = row * COLS + col
            for source, target, frame in ((low_ref, to_low_ref, 0), (high_ref, to_high_ref, 3)):
                key_grad, value_grad = finish(source, index, frame, row, col)
                target[index, 0] = key_grad.astype(BF16)
                target[index, 1] = value_grad.astype(BF16)
            for frame in (1, 2):
                here = (frame - 1) * HALF + index
                key_grad, value_grad = finish(kv_ref, here, frame, row, col)
                own_ref[here, 0] = key_grad
                own_ref[here, 1] = value_grad

    owner = flags_ref[2] > 0
    lines = []
    for first in (0, 8):
        line = jnp.sum(gains[first : first + 8], axis=0, keepdims=True)
        line = jnp.where(owner, line, 0.0)
        for _ in range(3):
            rounded = line.astype(BF16).astype(F32)
            lines.append(rounded)
            line = line - rounded
    lines.append(jnp.zeros((EXTRA - 6, HD), F32))
    block = jnp.concatenate(lines, axis=0).astype(BF16)
    for index in range(GROUP):
        dq_ref[index, PAIR : PAIR + EXTRA] = block


def attention(flags, kv, low, high, qd, q_gain, k_gain):
    rows = WIDE * COLUMN
    vmem = pl.BlockSpec(memory_space=pltpu.VMEM)
    products = 5 * 44 * SLAB * SLAB * 6 * HD
    return pl.pallas_call(
        attention_kernel,
        in_specs=[pl.BlockSpec(memory_space=pltpu.SMEM)] + [vmem] * 6,
        out_specs=[vmem] * 4,
        out_shape=[
            jax.ShapeDtypeStruct((GROUP, PAIR + EXTRA, HD), BF16),
            jax.ShapeDtypeStruct((GROUP, 2, PAIR, HD), F32),
            jax.ShapeDtypeStruct((HALF, 2, PAIR, HD), BF16),
            jax.ShapeDtypeStruct((HALF, 2, PAIR, HD), BF16),
        ],
        scratch_shapes=[
            pltpu.VMEM((rows, HD), BF16),
            pltpu.VMEM((HD, rows), BF16),
            pltpu.VMEM((rows, HD), BF16),
            pltpu.VMEM((rows // 2, HD), BF16),
            pltpu.VMEM((rows // 2, HD), BF16),
            pltpu.VMEM((rows, HD), F32),
            pltpu.VMEM((rows, HD), F32),
            pltpu.VMEM((16, HD), F32),
        ],
        name="attention",
        cost_estimate=pl.CostEstimate(flops=products, bytes_accessed=8 << 20, transcendentals=4 << 20),
        compiler_params=pltpu.CompilerParams(vmem_limit_bytes=VMEM_BYTES),
    )(flags, kv, low, high, qd, q_gain, k_gain)


def finish_kernel(kv_ref, own_ref, low_ref, high_ref, k_gain_ref, out_ref):
    k_gain = k_gain_ref[...]
    for index in range(GROUP):
        arrived = low_ref if index < HALF else high_ref
        raw = kv_ref[index, 0].astype(F32)
        key_grad = own_ref[index, 0] + arrived[index % HALF, 0].astype(F32)
        value_grad = own_ref[index, 1] + arrived[index % HALF, 1].astype(F32)
        out_ref[index, 0] = norm_back(raw, inverse_rms(raw), k_gain, key_grad).astype(BF16)
        out_ref[index, 1] = value_grad.astype(BF16)


def finish(kv, own, low, high, k_gain):
    return pl.pallas_call(
        finish_kernel,
        out_shape=jax.ShapeDtypeStruct((GROUP, 2, PAIR, HD), BF16),
        name="finish",
        compiler_params=pltpu.CompilerParams(vmem_limit_bytes=VMEM_BYTES),
    )(kv, own, low, high, k_gain)


def unpack_query_kernel(in_ref, out_ref, gains_ref):
    for head in range(HEADS):
        out_ref[0, :, head * HD : (head + 1) * HD] = in_ref[head, :PAIR]
    total = in_ref[0, PAIR : PAIR + EXTRA].astype(F32)
    for index in range(1, GROUP):
        total = total + in_ref[index, PAIR : PAIR + EXTRA].astype(F32)
    gains_ref[...] = total


def unpack_query(arrived):
    return pl.pallas_call(
        unpack_query_kernel,
        out_shape=[
            jax.ShapeDtypeStruct((1, PAIR, HEADS * HD), BF16),
            jax.ShapeDtypeStruct((EXTRA, HD), F32),
        ],
        name="unpack_query",
        compiler_params=pltpu.CompilerParams(vmem_limit_bytes=VMEM_BYTES),
    )(arrived)


def unpack_kernel(in_ref, key_ref, value_ref):
    for head in range(HEADS):
        key_ref[0, :, head * HD : (head + 1) * HD] = in_ref[head, 0]
        value_ref[0, :, head * HD : (head + 1) * HD] = in_ref[head, 1]


def unpack(arrived):
    return pl.pallas_call(
        unpack_kernel,
        out_shape=[jax.ShapeDtypeStruct((1, PAIR, HEADS * HD), BF16)] * 2,
        name="unpack",
        compiler_params=pltpu.CompilerParams(vmem_limit_bytes=VMEM_BYTES),
    )(arrived)


def swap(array, axis):
    return lax.all_to_all(array, axis, 0, 0)


def on_device(blocks, q_raw, k_raw, values, d_out, q_gain, k_gain):
    block = lax.axis_index("x")
    member = lax.axis_index("g")
    flags = jnp.stack([block > 0, block < blocks - 1, member < HEADS]).astype(jnp.int32)
    up = [(source, source + 1) for source in range(blocks - 1)]
    down = [(source + 1, source) for source in range(blocks - 1)]
    q_line = q_gain.reshape(1, HD)
    k_line = k_gain.reshape(1, HD)

    kv = swap(pack(k_raw, values), "g")
    low = lax.ppermute(kv[HALF:], "x", up)
    high = lax.ppermute(kv[:HALF], "x", down)
    qd = swap(pack(q_raw, d_out), "g")
    dq, own, to_low, to_high = attention(flags, kv, low, high, qd, q_line, k_line)
    from_low = lax.ppermute(to_high, "x", up)
    from_high = lax.ppermute(to_low, "x", down)
    q_grad, sums = unpack_query(swap(dq, "g"))
    grads = finish(kv, own, from_low, from_high, k_line)
    k_grad, v_grad = unpack(swap(grads, "g"))
    sums = jnp.stack([jnp.sum(sums[0:3], axis=0), jnp.sum(sums[3:6], axis=0)])
    count = lax.axis_size("dp") * blocks
    sums = swap(jnp.broadcast_to(sums[None], (count, 2, HD)), ("dp", "x"))
    sums = jnp.sum(sums, axis=0)
    return (q_grad, k_grad, v_grad, sums[0], sums[1])


def solution(mesh):
    videos, seq = mesh.devices.shape
    blocks = seq // GROUP
    split = Mesh(mesh.devices.reshape(videos, blocks, GROUP), ("dp", "x", "g"))
    tokens = P("dp", ("x", "g"), None)
    return jax.shard_map(
        functools.partial(on_device, blocks),
        mesh=split,
        in_specs=(tokens, tokens, tokens, tokens, P(), P()),
        out_specs=(tokens, tokens, tokens, P(), P()),
        check_vma=False,
    )
```

```python
import functools

import jax
import jax.numpy as jnp
from jax import lax
from jax.experimental import pallas as pl
from jax.experimental.pallas import tpu as pltpu
from jax.sharding import Mesh
from jax.sharding import PartitionSpec as P

HEADS = 12
HD = 128
TILE = 64
PAIR = 2 * TILE
GROUP = 16
HALF = 8
COLS = 4
EXTRA = 16
WIDE = 8
EPSILON = 1e-06
SCALE = HD ** (-0.5)
SCALE_LOG2E = SCALE * 1.4426950408889634
F32 = jnp.float32
BF16 = jnp.bfloat16
MIB = 1024 * 1024


def nt(left, right):
    return lax.dot_general(left, right, (((1,), (1,)), ((), ())), preferred_element_type=F32)


def nn(left, right):
    return lax.dot_general(left, right, (((1,), (0,)), ((), ())), preferred_element_type=F32)


def inverse_rms(inputs):
    return lax.rsqrt(jnp.mean(inputs * inputs, axis=-1, keepdims=True) + EPSILON)


def norm_back(inputs, inverse, gain, cotangent):
    scaled = cotangent * gain
    mean = jnp.mean(inputs * scaled, axis=-1, keepdims=True)
    return inverse * scaled - inputs * (inverse * inverse * inverse * mean)


def call(kernel, name, out_shape, arguments, flags=False, scratch=(), flops=0, limit=60):
    vmem = pl.BlockSpec(memory_space=pltpu.VMEM)
    in_specs = [vmem] * len(arguments)
    if flags:
        in_specs[0] = pl.BlockSpec(memory_space=pltpu.SMEM)
    return pl.pallas_call(
        kernel,
        in_specs=in_specs,
        out_specs=[vmem] * len(out_shape),
        out_shape=[jax.ShapeDtypeStruct(shape, dtype) for shape, dtype in out_shape],
        scratch_shapes=list(scratch),
        name=name,
        cost_estimate=pl.CostEstimate(flops=flops, bytes_accessed=4 * MIB, transcendentals=0),
        compiler_params=pltpu.CompilerParams(vmem_limit_bytes=limit * MIB),
    )(*arguments)


def pack_kernel(k_ref, v_ref, q_ref, d_ref, kv_ref, qd_ref, sem):
    copies = []
    for target, sources in ((kv_ref, (k_ref, v_ref)), (qd_ref, (q_ref, d_ref))):
        for head in range(HEADS):
            lanes = pl.ds(head * HD, HD)
            for number, source in enumerate(sources):
                copies.append(pltpu.make_async_copy(source.at[0, :, lanes], target.at[head, number], sem))
    for copy in copies:
        copy.start()
    for target in (kv_ref, qd_ref):
        for head in range(HEADS, GROUP):
            target[head] = jnp.zeros(target.shape[1:], target.dtype)
    for copy in copies:
        copy.wait()


def pack(*sources):
    out = jax.ShapeDtypeStruct((GROUP, 2, PAIR, HD), BF16)
    return pl.pallas_call(
        pack_kernel,
        in_specs=[pl.BlockSpec(memory_space=pl.ANY)] * 4,
        out_specs=[pl.BlockSpec(memory_space=pltpu.VMEM)] * 2,
        out_shape=[out, out],
        scratch_shapes=[pltpu.SemaphoreType.DMA],
        name="pack",
        compiler_params=pltpu.CompilerParams(vmem_limit_bytes=60 * MIB),
    )(*sources)


def blocks_of(frames):
    for frame in range(frames):
        for row in range(2):
            for col in range(COLS):
                yield frame * HALF + row * COLS + col, frame, row, col


def spread(parts):
    return parts[0] + jnp.concatenate(parts[1:], axis=1)


def raw_column(source, w, frame):
    place = slice((w % 2) * TILE, (w % 2 + 1) * TILE)
    index = frame * HALF + w // 2
    return jnp.concatenate([source[index, 0, place], source[index + COLS, 0, place]], axis=0).astype(F32)


def attention_kernel(
    flags_ref,
    kv_ref,
    low_ref,
    high_ref,
    qd_ref,
    q_gain_ref,
    k_gain_ref,
    dq_ref,
    own_ref,
    to_low,
    to_high,
    kn_own,
    knt_own,
    vv_own,
    kn_l,
    knt_l,
    vv_l,
    kn_h,
    knt_h,
    vv_h,
    qn,
    dd,
    q_side,
    d_side,
    chance_own,
    chance_l,
    chance_h,
    score_own,
    score_l,
    score_h,
    gains_ref,
):
    q_gain = q_gain_ref[...]
    k_gain = k_gain_ref[...]
    def prepare(col):
        for source, frames, kn, knt, vv in (
            (kv_ref, 2, kn_own, knt_own, vv_own),
            (low_ref, 1, kn_l, knt_l, vv_l),
            (high_ref, 1, kn_h, knt_h, vv_h),
        ):
            for frame in range(frames):
                for row in range(2):
                    index = frame * HALF + row * COLS + col
                    raw = source[index, 0].astype(F32)
                    normed = (raw * inverse_rms(raw) * k_gain).astype(BF16)
                    for part in range(2):
                        at = ((2 * col + part) * frames + frame) * PAIR + row * TILE
                        kn[at : at + TILE] = normed[part * TILE : (part + 1) * TILE]
                        vv[at : at + TILE] = source[index, 1, part * TILE : (part + 1) * TILE]
            for block in range(2 * col * frames, 2 * (col + 1) * frames):
                rows = slice(block * PAIR, (block + 1) * PAIR)
                knt[:, rows] = kn[rows].T
        for frame in range(2):
            for row in range(2):
                index = frame * HALF + row * COLS + col
                raw = qd_ref[index, 0].astype(F32)
                normed = (raw * inverse_rms(raw) * q_gain).astype(BF16)
                for part in range(2):
                    place = slice(part * TILE, (part + 1) * TILE)
                    at = ((2 * col + part) * 2 + frame) * PAIR + row * TILE
                    qn[at : at + TILE] = normed[place]
                    dd[at : at + TILE] = qd_ref[index, 1, place]
                    at = (2 * col + part) * PAIR + row * TILE
                    q_side[frame, at : at + TILE] = normed[place]
                    d_side[frame, at : at + TILE] = qd_ref[index, 1, place]

    gains_ref[...] = jnp.zeros_like(gains_ref)
    sources = (
        (kn_own, knt_own, vv_own, chance_own, score_own, 2, 0, 2 * PAIR, None),
        (kn_l, knt_l, vv_l, chance_l, score_l, 1, 0, PAIR, flags_ref[0].astype(F32)),
        (kn_h, knt_h, vv_h, chance_h, score_h, 1, PAIR, PAIR, flags_ref[1].astype(F32)),
    )

    def first_half(w, before, count):
        q_rows = pl.ds(w * (2 * PAIR), 2 * PAIR)
        q_tile = qn[q_rows]
        d_tile = dd[q_rows]
        weights, weight_grads, sums = [], [], []
        for kn, _, vv, _, _, frames, first, width, valid in sources:
            rows = pl.ds((w - before) * (frames * PAIR), count * frames * PAIR)
            queries = slice(first, first + width)
            weight = jnp.exp2(nt(kn[rows], q_tile[queries]) * SCALE_LOG2E)
            if valid is not None:
                weight = weight * valid
            weights.append(weight)
            sums.append(jnp.sum(weight, axis=0, keepdims=True))
            weight_grads.append(nt(vv[rows], d_tile[queries]))
        return q_tile, d_tile, weights, weight_grads, sums

    def second_half(w, before, count, q_tile, d_tile, weights, weight_grads, sums):
        reciprocal = 1.0 / spread(sums)
        chances, dots = [], []
        for number, (_, _, _, store, _, frames, first, width, _) in enumerate(sources):
            chance = weights[number] * reciprocal[:, first : first + width]
            rounded = chance.astype(BF16)
            dots.append(jnp.sum(rounded.astype(F32) * weight_grads[number], axis=0, keepdims=True))
            chances.append(chance)
            for step in range(count):
                place = (1 - (step - before)) * width
                store[w - before + step, :, place : place + width] = rounded[
                    step * frames * PAIR : (step + 1) * frames * PAIR
                ]
        row_dot = spread(dots)
        grads = []
        for number, (_, knt, _, _, store, frames, first, width, _) in enumerate(sources):
            score = chances[number] * (weight_grads[number] - row_dot[:, first : first + width])
            score = score.astype(BF16)
            for step in range(count):
                place = (1 - (step - before)) * width
                store[w - before + step, :, place : place + width] = score[
                    step * frames * PAIR : (step + 1) * frames * PAIR
                ]
            lanes = pl.ds((w - before) * (frames * PAIR), count * frames * PAIR)
            grads.append(nn(knt[:, lanes], score))
        grad = spread(grads).T * SCALE
        col = w // 2
        place = pl.ds((w % 2) * TILE, TILE)
        for frame in range(2):
            for row in range(2):
                index = frame * HALF + row * COLS + col
                raw = qd_ref[index, 0, place].astype(F32)
                inverse = inverse_rms(raw)
                part = grad[frame * PAIR + row * TILE : frame * PAIR + (row + 1) * TILE]
                gains_ref[...] += jnp.sum((part * raw * inverse).reshape(-1, 8, HD), axis=0)
                dq_ref[index, place] = norm_back(raw, inverse, q_gain, part).astype(BF16)

    def key_sums(chance, score, queries, cotangents, w, width):
        first, last = max(w - 1, 0), min(w + 1, WIDE - 1)
        lanes = slice((first - w + 1) * width, (last - w + 2) * width)
        rows = slice(first * width, (last + 1) * width)
        value_grad = nn(chance[w, :, lanes], cotangents[rows])
        key_grad = nn(score[w, :, lanes], queries[rows]) * SCALE
        return key_grad, value_grad

    def gain_part(key_grad, raw):
        return jnp.sum((key_grad * raw * inverse_rms(raw)).reshape(-1, 8, HD), axis=0)

    sides = ((chance_l, score_l, low_ref, to_low), (chance_h, score_h, high_ref, to_high))

    def key_column(w, gain_sum):
        for frame, (chance, score, raw_ref, out_ref) in enumerate(sides):
            key_grad, value_grad = key_sums(chance, score, q_side.at[frame], d_side.at[frame], w, PAIR)
            out_ref[w, 0] = key_grad.astype(BF16)
            out_ref[w, 1] = value_grad.astype(BF16)
            gain_sum += gain_part(key_grad, raw_column(raw_ref, w, 0))
        key_grad, value_grad = key_sums(chance_own, score_own, qn, dd, w, 2 * PAIR)
        own_ref[w, 0] = key_grad
        own_ref[w, 1] = value_grad
        for frame in range(2):
            gain_sum += gain_part(key_grad[frame * PAIR : (frame + 1) * PAIR], raw_column(kv_ref, w, frame))
        return gain_sum

    def extent(w):
        return w, min(w, 1), 2 if w in (0, WIDE - 1) else 3

    gain_sum = jnp.zeros((8, HD), F32)
    prepare(0)
    held = first_half(*extent(0))
    for w in range(WIDE):
        if w % 2 == 0 and w // 2 + 1 < COLS:
            prepare(w // 2 + 1)
        following = first_half(*extent(w + 1)) if w + 1 < WIDE else None
        second_half(*extent(w), *held)
        held = following
        if w > 0:
            gain_sum = key_column(w - 1, gain_sum)
    gain_sum = key_column(WIDE - 1, gain_sum)


    q_sum = jnp.sum(gains_ref[...], axis=0, keepdims=True)
    k_sum = jnp.sum(gain_sum, axis=0, keepdims=True)
    lines = []
    for line in (q_sum, k_sum):
        line = jnp.where(flags_ref[2] > 0, line, 0.0)
        for _ in range(3):
            rounded = line.astype(BF16).astype(F32)
            lines.append(rounded)
            line = line - rounded
    lines.append(jnp.zeros((EXTRA - 6, HD), F32))
    block = jnp.concatenate(lines, axis=0).astype(BF16)
    for index in range(GROUP):
        dq_ref[index, PAIR : PAIR + EXTRA] = block


def attention(flags, kv, low, high, qd, q_gain, k_gain):
    own, halo = WIDE * 2 * PAIR, WIDE * PAIR
    scratch = []
    for rows in (own, halo, halo):
        scratch += [pltpu.VMEM((rows, HD), BF16), pltpu.VMEM((HD, rows), BF16), pltpu.VMEM((rows, HD), BF16)]
    scratch += [pltpu.VMEM((own, HD), BF16)] * 2 + [pltpu.VMEM((2, halo, HD), BF16)] * 2
    stores = [pltpu.VMEM((WIDE, 2 * PAIR, 6 * PAIR), BF16)] + [pltpu.VMEM((WIDE, PAIR, 3 * PAIR), BF16)] * 2
    scratch += stores + stores + [pltpu.VMEM((8, HD), F32)]
    to_side = ((WIDE, 2, PAIR, HD), BF16)
    out_shape = [((GROUP, PAIR + EXTRA, HD), BF16), ((WIDE, 2, 2 * PAIR, HD), F32), to_side, to_side]
    return call(
        attention_kernel,
        "attention",
        out_shape,
        (flags, kv, low, high, qd, q_gain, k_gain),
        flags=True,
        scratch=scratch,
        flops=5 * 66 * PAIR * PAIR * PAIR * 2,
        limit=60,
    )


def finish_kernel(kv_ref, own_ref, low_ref, high_ref, k_gain_ref, out_ref):
    k_gain = k_gain_ref[...]
    for w in range(WIDE):
        place = slice((w % 2) * TILE, (w % 2 + 1) * TILE)
        for frame, arrived in enumerate((low_ref, high_ref)):
            rows = slice(frame * PAIR, (frame + 1) * PAIR)
            raw = raw_column(kv_ref, w, frame)
            key_grad = own_ref[w, 0, rows] + arrived[w, 0].astype(F32)
            value_grad = (own_ref[w, 1, rows] + arrived[w, 1].astype(F32)).astype(BF16)
            key_grad = norm_back(raw, inverse_rms(raw), k_gain, key_grad).astype(BF16)
            for row in range(2):
                index = frame * HALF + row * COLS + w // 2
                out_ref[index, 0, place] = key_grad[row * TILE : (row + 1) * TILE]
                out_ref[index, 1, place] = value_grad[row * TILE : (row + 1) * TILE]


def finish(kv, own, low, high, k_gain):
    out_shape = [((GROUP, 2, PAIR, HD), BF16)]
    return call(finish_kernel, "finish", out_shape, (kv, own, low, high, k_gain))[0]


def unpack_query_kernel(in_ref, out_ref, lines_ref):
    for head in range(HEADS):
        out_ref[0, :, head * HD : (head + 1) * HD] = in_ref[head, :PAIR]
    total = in_ref[0, PAIR : PAIR + EXTRA].astype(F32)
    for index in range(1, GROUP):
        total = total + in_ref[index, PAIR : PAIR + EXTRA].astype(F32)
    sums = [jnp.sum(total[first : first + 3], axis=0, keepdims=True) for first in (0, 3)]
    lines_ref[...] = jnp.concatenate(sums + [jnp.zeros((6, HD), F32)], axis=0)


def unpack_kernel(in_ref, key_ref, value_ref):
    for head in range(HEADS):
        key_ref[0, :, head * HD : (head + 1) * HD] = in_ref[head, 0]
        value_ref[0, :, head * HD : (head + 1) * HD] = in_ref[head, 1]


def swap(array):
    return lax.all_to_all(array, "g", 0, 0)


def sum_over(lines, axis, steps):
    count = lax.axis_size(axis)
    total = lines
    for step in steps:
        total = total + lax.ppermute(lines, axis, [(source, source ^ step) for source in range(count)])
    return total


def on_device(blocks, q_raw, k_raw, values, d_out, q_gain, k_gain):
    block = lax.axis_index("x")
    member = lax.axis_index("g")
    flags = jnp.stack([block > 0, block < blocks - 1, member < HEADS]).astype(jnp.int32)
    up = [(source, source + 1) for source in range(blocks - 1)]
    down = [(source + 1, source) for source in range(blocks - 1)]
    q_line = q_gain.reshape(1, HD)
    k_line = k_gain.reshape(1, HD)
    tokens = ((1, PAIR, HEADS * HD), BF16)

    kv, qd = pack(k_raw, values, q_raw, d_out)
    kv = swap(kv)
    low = lax.ppermute(kv[HALF:], "x", up)
    high = lax.ppermute(kv[:HALF], "x", down)
    qd = swap(qd)
    dq, own, to_low, to_high = attention(flags, kv, low, high, qd, q_line, k_line)
    arrived = swap(dq)
    from_low = lax.ppermute(to_high, "x", up)
    from_high = lax.ppermute(to_low, "x", down)
    q_grad, lines = call(unpack_query_kernel, "unpack_query", [tokens, ((8, HD), F32)], (arrived,))
    grads = finish(kv, own, from_low, from_high, k_line)
    k_grad, v_grad = call(unpack_kernel, "unpack", [tokens, tokens], (swap(grads),))
    lines = sum_over(lines, "dp", (1, 2, 3))
    lines = sum_over(lines, "x", (1, 2, 3))
    return (q_grad, k_grad, v_grad, lines[0], lines[1])


def solution(mesh):
    videos, seq = mesh.devices.shape
    blocks = seq // GROUP
    split = Mesh(mesh.devices.reshape(videos, blocks, GROUP), ("dp", "x", "g"))
    tokens = P("dp", ("x", "g"), None)
    return jax.shard_map(
        functools.partial(on_device, blocks),
        mesh=split,
        in_specs=(tokens, tokens, tokens, tokens, P(), P()),
        out_specs=(tokens, tokens, tokens, P(), P()),
        check_vma=False,
    )
```

```python
import functools

import jax
import jax.numpy as jnp
from jax import lax
from jax.experimental import pallas as pl
from jax.experimental.pallas import tpu as pltpu
from jax.sharding import Mesh
from jax.sharding import PartitionSpec as P

HEADS = 12
HD = 128
TILE = 64
PAIR = 2 * TILE
GROUP = 16
HALF = 8
COLS = 4
EXTRA = 16
WIDE = 8
EPSILON = 1e-06
SCALE = HD ** (-0.5)
SCALE_LOG2E = SCALE * 1.4426950408889634
F32 = jnp.float32
BF16 = jnp.bfloat16
LIMIT = 60 * 1024 * 1024
SMALL = 8 * 1024 * 1024
FINISH_LIMIT = 52 * 1024 * 1024


def nt(left, right):
    return lax.dot_general(left, right, (((1,), (1,)), ((), ())), preferred_element_type=F32)


def nn(left, right):
    return lax.dot_general(left, right, (((1,), (0,)), ((), ())), preferred_element_type=F32)


def inverse_rms(inputs):
    return lax.rsqrt(jnp.mean(inputs * inputs, axis=-1, keepdims=True) + EPSILON)


def norm_back(inputs, inverse, gain, cotangent):
    scaled = cotangent * gain
    mean = jnp.mean(inputs * scaled, axis=-1, keepdims=True)
    return inverse * scaled - inputs * (inverse * inverse * inverse * mean)


def pack_kernel(first_ref, second_ref, out_ref, sem):
    copies = []
    for head in range(HEADS):
        lanes = pl.ds(head * HD, HD)
        for number, source in enumerate((first_ref, second_ref)):
            copies.append(pltpu.make_async_copy(source.at[0, :, lanes], out_ref.at[head, number], sem))
    for copy in copies:
        copy.start()
    for head in range(HEADS, GROUP):
        out_ref[head] = jnp.zeros(out_ref.shape[1:], out_ref.dtype)
    for copy in copies:
        copy.wait()


def pack(first, second):
    return pl.pallas_call(
        pack_kernel,
        in_specs=[pl.BlockSpec(memory_space=pl.ANY)] * 2,
        out_specs=pl.BlockSpec(memory_space=pltpu.VMEM),
        out_shape=jax.ShapeDtypeStruct((GROUP, 2, PAIR, HD), BF16),
        scratch_shapes=[pltpu.SemaphoreType.DMA],
        name="pack",
        compiler_params=pltpu.CompilerParams(vmem_limit_bytes=LIMIT),
    )(first, second)


def spread(parts):
    return parts[0] + jnp.concatenate(parts[1:], axis=1)


def raw_column(source, w, frame, col):
    place = slice((w % 2) * TILE, (w % 2 + 1) * TILE)
    rows = [source[frame, row, col, 0, place] for row in range(2)]
    return jnp.concatenate(rows, axis=0).astype(F32)


def attention_kernel(
    flags_ref,
    kv_hbm,
    low_hbm,
    high_hbm,
    qd_hbm,
    q_gain_ref,
    k_gain_ref,
    dq_hbm,
    own_hbm,
    to_low_hbm,
    to_high_hbm,
    kv_ref,
    low_ref,
    high_ref,
    qd_ref,
    dq_ref,
    own_ref,
    to_low,
    to_high,
    in_sems,
    out_sem,
    kn_own,
    knt_own,
    vv_own,
    kn_l,
    knt_l,
    vv_l,
    kn_h,
    knt_h,
    vv_h,
    qn,
    dd,
    q_side,
    d_side,
    chance_own,
    chance_l,
    chance_h,
    score_own,
    score_l,
    score_h,
    gains_ref,
):
    arrivals = []
    for col in range(COLS):
        pairs = ((kv_hbm, kv_ref), (low_hbm, low_ref), (high_hbm, high_ref), (qd_hbm, qd_ref))
        copies = [
            pltpu.make_async_copy(source.at[:, :, col], target.at[:, :, col], in_sems.at[col])
            for source, target in pairs
        ]
        for copy in copies:
            copy.start()
        arrivals.append(copies)
    departures = []

    def send(source, target):
        copy = pltpu.make_async_copy(source, target, out_sem)
        copy.start()
        departures.append(copy)

    q_gain = q_gain_ref[...]
    k_gain = k_gain_ref[...]
    def prepare(col):
        for copy in arrivals[col]:
            copy.wait()
        for source, frames, kn, knt, vv in (
            (kv_ref, 2, kn_own, knt_own, vv_own),
            (low_ref, 1, kn_l, knt_l, vv_l),
            (high_ref, 1, kn_h, knt_h, vv_h),
        ):
            for frame in range(frames):
                for row in range(2):
                    raw = source[frame, row, col, 0].astype(F32)
                    normed = (raw * inverse_rms(raw) * k_gain).astype(BF16)
                    for part in range(2):
                        at = ((2 * col + part) * frames + frame) * PAIR + row * TILE
                        kn[at : at + TILE] = normed[part * TILE : (part + 1) * TILE]
                        vv[at : at + TILE] = source[frame, row, col, 1, part * TILE : (part + 1) * TILE]
            for block in range(2 * col * frames, 2 * (col + 1) * frames):
                rows = slice(block * PAIR, (block + 1) * PAIR)
                knt[:, rows] = kn[rows].T
        for frame in range(2):
            for row in range(2):
                raw = qd_ref[frame, row, col, 0].astype(F32)
                normed = (raw * inverse_rms(raw) * q_gain).astype(BF16)
                for part in range(2):
                    place = slice(part * TILE, (part + 1) * TILE)
                    at = ((2 * col + part) * 2 + frame) * PAIR + row * TILE
                    qn[at : at + TILE] = normed[place]
                    dd[at : at + TILE] = qd_ref[frame, row, col, 1, place]
                    at = (2 * col + part) * PAIR + row * TILE
                    q_side[frame, at : at + TILE] = normed[place]
                    d_side[frame, at : at + TILE] = qd_ref[frame, row, col, 1, place]

    gains_ref[...] = jnp.zeros_like(gains_ref)
    sources = (
        (kn_own, knt_own, vv_own, chance_own, score_own, 2, 0, 2 * PAIR, None),
        (kn_l, knt_l, vv_l, chance_l, score_l, 1, 0, PAIR, flags_ref[0].astype(F32)),
        (kn_h, knt_h, vv_h, chance_h, score_h, 1, PAIR, PAIR, flags_ref[1].astype(F32)),
    )

    def first_half(w, before, count):
        q_rows = pl.ds(w * (2 * PAIR), 2 * PAIR)
        q_tile = qn[q_rows]
        d_tile = dd[q_rows]
        weights, weight_grads, sums = [], [], []
        for kn, _, vv, _, _, frames, first, width, valid in sources:
            rows = pl.ds((w - before) * (frames * PAIR), count * frames * PAIR)
            queries = slice(first, first + width)
            weight = jnp.exp2(nt(kn[rows], q_tile[queries]) * SCALE_LOG2E)
            if valid is not None:
                weight = weight * valid
            weights.append(weight)
            sums.append(jnp.sum(weight, axis=0, keepdims=True))
            weight_grads.append(nt(vv[rows], d_tile[queries]))
        return q_tile, d_tile, weights, weight_grads, sums

    def second_half(w, before, count, q_tile, d_tile, weights, weight_grads, sums):
        reciprocal = 1.0 / spread(sums)
        chances, dots = [], []
        for number, (_, _, _, store, _, frames, first, width, _) in enumerate(sources):
            chance = weights[number] * reciprocal[:, first : first + width]
            rounded = chance.astype(BF16)
            dots.append(jnp.sum(rounded.astype(F32) * weight_grads[number], axis=0, keepdims=True))
            chances.append(chance)
            for step in range(count):
                place = (1 - (step - before)) * width
                store[w - before + step, :, place : place + width] = rounded[
                    step * frames * PAIR : (step + 1) * frames * PAIR
                ]
        row_dot = spread(dots)
        grads = []
        for number, (_, knt, _, _, store, frames, first, width, _) in enumerate(sources):
            score = chances[number] * (weight_grads[number] - row_dot[:, first : first + width])
            score = score.astype(BF16)
            for step in range(count):
                place = (1 - (step - before)) * width
                store[w - before + step, :, place : place + width] = score[
                    step * frames * PAIR : (step + 1) * frames * PAIR
                ]
            lanes = pl.ds((w - before) * (frames * PAIR), count * frames * PAIR)
            grads.append(nn(knt[:, lanes], score))
        grad = spread(grads).T * SCALE
        col = w // 2
        place = pl.ds((w % 2) * TILE, TILE)
        for frame in range(2):
            for row in range(2):
                raw = qd_ref[frame, row, col, 0, place].astype(F32)
                inverse = inverse_rms(raw)
                part = grad[frame * PAIR + row * TILE : frame * PAIR + (row + 1) * TILE]
                gains_ref[...] += jnp.sum((part * raw * inverse).reshape(-1, 8, HD), axis=0)
                dq_ref[frame, row, col, place] = norm_back(raw, inverse, q_gain, part).astype(BF16)
        if w % 2:
            send(dq_ref.at[:, :, col, :PAIR], dq_hbm.at[:, :, col, :PAIR])

    def key_sums(chance, score, queries, cotangents, w, width):
        first, last = max(w - 1, 0), min(w + 1, WIDE - 1)
        lanes = slice((first - w + 1) * width, (last - w + 2) * width)
        rows = slice(first * width, (last + 1) * width)
        value_grad = nn(chance[w, :, lanes], cotangents[rows])
        key_grad = nn(score[w, :, lanes], queries[rows]) * SCALE
        return key_grad, value_grad

    def gain_part(key_grad, raw):
        return jnp.sum((key_grad * raw * inverse_rms(raw)).reshape(-1, 8, HD), axis=0)

    sides = (
        (chance_l, score_l, low_ref, to_low, to_low_hbm),
        (chance_h, score_h, high_ref, to_high, to_high_hbm),
    )

    def key_column(w, gain_sum):
        for frame, (chance, score, raw_ref, out_ref, out_hbm) in enumerate(sides):
            key_grad, value_grad = key_sums(chance, score, q_side.at[frame], d_side.at[frame], w, PAIR)
            out_ref[w, 0] = key_grad.astype(BF16)
            out_ref[w, 1] = value_grad.astype(BF16)
            send(out_ref.at[w], out_hbm.at[w])
            gain_sum += gain_part(key_grad, raw_column(raw_ref, w, 0, w // 2))
        key_grad, value_grad = key_sums(chance_own, score_own, qn, dd, w, 2 * PAIR)
        own_ref[w, 0] = key_grad.astype(BF16)
        own_ref[w, 1] = value_grad.astype(BF16)
        for frame in range(2):
            gain_sum += gain_part(key_grad[frame * PAIR : (frame + 1) * PAIR], raw_column(kv_ref, w, frame, w // 2))
        send(own_ref.at[w], own_hbm.at[w])
        return gain_sum

    def extent(w):
        return w, min(w, 1), 2 if w in (0, WIDE - 1) else 3

    gain_sum = jnp.zeros((8, HD), F32)
    prepare(0)
    held = first_half(*extent(0))
    for w in range(WIDE):
        if w % 2 == 0 and w // 2 + 1 < COLS:
            prepare(w // 2 + 1)
        following = first_half(*extent(w + 1)) if w + 1 < WIDE else None
        second_half(*extent(w), *held)
        held = following
        if w > 0:
            gain_sum = key_column(w - 1, gain_sum)
    gain_sum = key_column(WIDE - 1, gain_sum)


    q_sum = jnp.sum(gains_ref[...], axis=0, keepdims=True)
    k_sum = jnp.sum(gain_sum, axis=0, keepdims=True)
    lines = []
    for line in (q_sum, k_sum):
        line = jnp.where(flags_ref[2] > 0, line, 0.0)
        for _ in range(3):
            rounded = line.astype(BF16).astype(F32)
            lines.append(rounded)
            line = line - rounded
    lines.append(jnp.zeros((EXTRA - 6, HD), F32))
    block = jnp.concatenate(lines, axis=0).astype(BF16)
    dq_ref[:, :, :, PAIR:] = jnp.broadcast_to(block, (2, 2, COLS, EXTRA, HD))
    send(dq_ref.at[:, :, :, PAIR:], dq_hbm.at[:, :, :, PAIR:])
    for copy in departures:
        copy.wait()


def grid_of(array):
    return array.reshape((-1, 2, COLS) + array.shape[1:])


def attention(flags, kv, low, high, qd, q_gain, k_gain):
    own, halo = WIDE * 2 * PAIR, WIDE * PAIR
    arrays = [grid_of(array) for array in (kv, low, high, qd)]
    outs = [((2, 2, COLS, PAIR + EXTRA, HD), BF16), ((WIDE, 2, 2 * PAIR, HD), BF16)]
    outs += [((WIDE, 2, PAIR, HD), BF16)] * 2
    scratch = [pltpu.VMEM(array.shape, BF16) for array in arrays]
    scratch += [pltpu.VMEM(*out) for out in outs]
    scratch += [pltpu.SemaphoreType.DMA((COLS,)), pltpu.SemaphoreType.DMA]
    for rows in (own, halo, halo):
        scratch += [pltpu.VMEM((rows, HD), BF16), pltpu.VMEM((HD, rows), BF16), pltpu.VMEM((rows, HD), BF16)]
    scratch += [pltpu.VMEM((own, HD), BF16)] * 2 + [pltpu.VMEM((2, halo, HD), BF16)] * 2
    stores = [pltpu.VMEM((WIDE, 2 * PAIR, 6 * PAIR), BF16)] + [pltpu.VMEM((WIDE, PAIR, 3 * PAIR), BF16)] * 2
    scratch += stores + stores + [pltpu.VMEM((8, HD), F32)]
    dq, own, to_low, to_high = pl.pallas_call(
        attention_kernel,
        in_specs=[pl.BlockSpec(memory_space=pltpu.SMEM)]
        + [pl.BlockSpec(memory_space=pl.ANY)] * 4
        + [pl.BlockSpec(memory_space=pltpu.VMEM)] * 2,
        out_specs=[pl.BlockSpec(memory_space=pl.ANY)] * 4,
        out_shape=[pltpu.HBM(*out) for out in outs],
        scratch_shapes=scratch,
        name="attention",
        cost_estimate=pl.CostEstimate(
            flops=5 * 66 * PAIR * PAIR * PAIR * 2, bytes_accessed=8 << 20, transcendentals=0
        ),
        compiler_params=pltpu.CompilerParams(vmem_limit_bytes=FINISH_LIMIT),
    )(flags, *arrays, q_gain, k_gain)
    return dq.reshape(GROUP, PAIR + EXTRA, HD), own, to_low, to_high


def finish_kernel(frame, kv_hbm, own_hbm, halo_hbm, k_gain_ref, out_hbm, kv_ref, own_ref, halo_ref, out_ref, in_sems, out_sem):
    rows = slice(frame * PAIR, (frame + 1) * PAIR)
    arrivals = []
    for col in range(COLS):
        columns = slice(2 * col, 2 * col + 2)
        pairs = (
            (halo_hbm.at[columns], halo_ref.at[columns]),
            (kv_hbm.at[frame, :, col], kv_ref.at[0, :, col]),
            (own_hbm.at[columns, :, rows], own_ref.at[columns]),
        )
        copies = [pltpu.make_async_copy(source, target, in_sems.at[col]) for source, target in pairs]
        for copy in copies:
            copy.start()
        arrivals.append(copies)
    k_gain = k_gain_ref[...]
    departures = []
    for col in range(COLS):
        for copy in arrivals[col]:
            copy.wait()
        for part in range(2):
            w = 2 * col + part
            place = slice(part * TILE, (part + 1) * TILE)
            raw = raw_column(kv_ref, w, 0, col)
            key_grad = own_ref[w, 0].astype(F32) + halo_ref[w, 0].astype(F32)
            value_grad = (own_ref[w, 1].astype(F32) + halo_ref[w, 1].astype(F32)).astype(BF16)
            key_grad = norm_back(raw, inverse_rms(raw), k_gain, key_grad).astype(BF16)
            for row in range(2):
                out_ref[row, col, 0, place] = key_grad[row * TILE : (row + 1) * TILE]
                out_ref[row, col, 1, place] = value_grad[row * TILE : (row + 1) * TILE]
        copy = pltpu.make_async_copy(out_ref.at[:, col], out_hbm.at[frame, :, col], out_sem)
        copy.start()
        departures.append(copy)
    for copy in departures:
        copy.wait()


def second_finish_kernel(kv_hbm, own_hbm, halo_hbm, k_gain_ref, first_hbm, *refs):
    finish_kernel(1, kv_hbm, own_hbm, halo_hbm, k_gain_ref, *refs)


def finish(frame, kv, own, halo, k_gain, first=None):
    half = (2, COLS, 2, PAIR, HD)
    arguments = [grid_of(kv), own, halo, k_gain]
    in_specs = [pl.BlockSpec(memory_space=pl.ANY)] * 3 + [pl.BlockSpec(memory_space=pltpu.VMEM)]
    aliases = {}
    if frame:
        arguments.append(first)
        in_specs.append(pl.BlockSpec(memory_space=pl.ANY))
        aliases = {4: 0}
    return pl.pallas_call(
        second_finish_kernel if frame else functools.partial(finish_kernel, 0),
        in_specs=in_specs,
        out_specs=pl.BlockSpec(memory_space=pl.ANY),
        out_shape=pltpu.HBM((2,) + half, BF16),
        scratch_shapes=[
            pltpu.VMEM((1,) + half, BF16),
            pltpu.VMEM((WIDE, 2, PAIR, HD), BF16),
            pltpu.VMEM((WIDE, 2, PAIR, HD), BF16),
            pltpu.VMEM(half, BF16),
            pltpu.SemaphoreType.DMA((COLS,)),
            pltpu.SemaphoreType.DMA,
        ],
        input_output_aliases=aliases,
        name="finish_high" if frame else "finish_low",
        compiler_params=pltpu.CompilerParams(vmem_limit_bytes=FINISH_LIMIT),
    )(*arguments)


def unpack_query_kernel(in_ref, out_ref, lines_ref):
    for head in range(HEADS):
        out_ref[0, :, head * HD : (head + 1) * HD] = in_ref[head, :PAIR]
    total = in_ref[0, PAIR:].astype(F32)
    for index in range(1, GROUP):
        total = total + in_ref[index, PAIR:].astype(F32)
    sums = [jnp.sum(total[first : first + 3], axis=0, keepdims=True) for first in (0, 3)]
    lines_ref[...] = jnp.concatenate(sums + [jnp.zeros((6, HD), F32)], axis=0)


def unpack_query(arrived):
    tokens = jax.ShapeDtypeStruct((1, PAIR, HEADS * HD), BF16)
    return pl.pallas_call(
        unpack_query_kernel,
        out_shape=[tokens, jax.ShapeDtypeStruct((8, HD), F32)],
        name="unpack_query",
        compiler_params=pltpu.CompilerParams(vmem_limit_bytes=SMALL),
    )(arrived)


def unpack_kernel(in_ref, key_ref, value_ref, sem):
    copies = []
    for head in range(HEADS):
        lanes = pl.ds(head * HD, HD)
        for number, target in enumerate((key_ref, value_ref)):
            copies.append(pltpu.make_async_copy(in_ref.at[head, number], target.at[0, :, lanes], sem))
    for copy in copies:
        copy.start()
    for copy in copies:
        copy.wait()


def unpack(arrived):
    out = pltpu.HBM((1, PAIR, HEADS * HD), BF16)
    return pl.pallas_call(
        unpack_kernel,
        in_specs=[pl.BlockSpec(memory_space=pltpu.VMEM)],
        out_specs=[pl.BlockSpec(memory_space=pl.ANY)] * 2,
        out_shape=[out, out],
        scratch_shapes=[pltpu.SemaphoreType.DMA],
        name="unpack",
        compiler_params=pltpu.CompilerParams(vmem_limit_bytes=SMALL),
    )(arrived)


def swap(array):
    return lax.all_to_all(array, "g", 0, 0)


def sum_over(lines, axis, steps):
    count = lax.axis_size(axis)
    total = lines
    for step in steps:
        total = total + lax.ppermute(lines, axis, [(source, source ^ step) for source in range(count)])
    return total


def on_device(blocks, q_raw, k_raw, values, d_out, q_gain, k_gain):
    block = lax.axis_index("x")
    member = lax.axis_index("g")
    flags = jnp.stack([block > 0, block < blocks - 1, member < HEADS]).astype(jnp.int32)
    up = [(source, source + 1) for source in range(blocks - 1)]
    down = [(source + 1, source) for source in range(blocks - 1)]
    q_line = q_gain.reshape(1, HD)
    k_line = k_gain.reshape(1, HD)

    kv = swap(pack(k_raw, values))
    low = lax.ppermute(kv[HALF:], "x", up)
    high = lax.ppermute(kv[:HALF], "x", down)
    qd = swap(pack(q_raw, d_out))
    dq, own, to_low, to_high = attention(flags, kv, low, high, qd, q_line, k_line)
    arrived = swap(dq)
    from_low = lax.ppermute(to_high, "x", up)
    from_high = lax.ppermute(to_low, "x", down)
    q_grad, lines = unpack_query(arrived)
    grads = finish(0, kv, own, from_low, k_line)
    grads = finish(1, kv, own, from_high, k_line, grads).reshape(GROUP, 2, PAIR, HD)
    k_grad, v_grad = unpack(swap(grads))
    lines = sum_over(lines, "dp", (1, 2, 3))
    lines = sum_over(lines, "x", (1, 2, 3))
    return (q_grad, k_grad, v_grad, lines[0], lines[1])


def solution(mesh):
    videos, seq = mesh.devices.shape
    blocks = seq // GROUP
    split = Mesh(mesh.devices.reshape(videos, blocks, GROUP), ("dp", "x", "g"))
    tokens = P("dp", ("x", "g"), None)
    return jax.shard_map(
        functools.partial(on_device, blocks),
        mesh=split,
        in_specs=(tokens, tokens, tokens, tokens, P(), P()),
        out_specs=(tokens, tokens, tokens, P(), P()),
        check_vma=False,
    )
```

```python
import functools

import jax
import jax.numpy as jnp
from jax import lax
from jax.experimental import pallas as pl
from jax.experimental.pallas import tpu as pltpu
from jax.sharding import Mesh
from jax.sharding import PartitionSpec as P

HEADS = 12
HD = 128
TILE = 64
PAIR = 2 * TILE
GROUP = 16
HALF = 8
COLS = 4
EXTRA = 16
WIDE = 8
EPSILON = 1e-06
SCALE = HD ** (-0.5)
SCALE_LOG2E = SCALE * 1.4426950408889634
F32 = jnp.float32
BF16 = jnp.bfloat16
LIMIT = 60 * 1024 * 1024
SMALL = 8 * 1024 * 1024
ATTENTION_LIMIT = 36 * 1024 * 1024


def nt(left, right):
    return lax.dot_general(left, right, (((1,), (1,)), ((), ())), preferred_element_type=F32)


def nn(left, right):
    return lax.dot_general(left, right, (((1,), (0,)), ((), ())), preferred_element_type=F32)


def inverse_rms(inputs):
    return lax.rsqrt(jnp.mean(inputs * inputs, axis=-1, keepdims=True) + EPSILON)


def norm_back(inputs, inverse, gain, cotangent):
    scaled = cotangent * gain
    mean = jnp.mean(inputs * scaled, axis=-1, keepdims=True)
    return inverse * scaled - inputs * (inverse * inverse * inverse * mean)


def pack_kernel(first_ref, second_ref, out_ref, sem):
    copies = []
    for head in range(HEADS):
        lanes = pl.ds(head * HD, HD)
        for number, source in enumerate((first_ref, second_ref)):
            copies.append(pltpu.make_async_copy(source.at[0, :, lanes], out_ref.at[head, number], sem))
    for copy in copies:
        copy.start()
    for head in range(HEADS, GROUP):
        out_ref[head] = jnp.zeros(out_ref.shape[1:], out_ref.dtype)
    for copy in copies:
        copy.wait()


def pack(first, second):
    return pl.pallas_call(
        pack_kernel,
        in_specs=[pl.BlockSpec(memory_space=pl.ANY)] * 2,
        out_specs=pl.BlockSpec(memory_space=pltpu.VMEM),
        out_shape=jax.ShapeDtypeStruct((GROUP, 2, PAIR, HD), BF16),
        scratch_shapes=[pltpu.SemaphoreType.DMA],
        name="pack",
        compiler_params=pltpu.CompilerParams(vmem_limit_bytes=LIMIT),
    )(first, second)


def spread(parts):
    return parts[0] + jnp.concatenate(parts[1:], axis=1)


def raw_column(source, w, frame, col):
    place = slice((w % 2) * TILE, (w % 2 + 1) * TILE)
    rows = [source[frame, row, col, 0, place] for row in range(2)]
    return jnp.concatenate(rows, axis=0).astype(F32)


def key_sums(chance, score, queries, cotangents, w, width):
    first, last = max(w - 1, 0), min(w + 1, WIDE - 1)
    lanes = slice((first - w + 1) * width, (last - w + 2) * width)
    rows = slice(first * width, (last + 1) * width)
    value_grad = nn(chance[w, :, lanes], cotangents[rows])
    key_grad = nn(score[w, :, lanes], queries[rows]) * SCALE
    return key_grad, value_grad


def attention_kernel(
    flags_ref,
    kv_hbm,
    low_hbm,
    high_hbm,
    qd_hbm,
    q_gain_ref,
    k_gain_ref,
    dq_hbm,
    to_low_hbm,
    to_high_hbm,
    qn_hbm,
    dd_hbm,
    chance_hbm,
    score_hbm,
    kv_ref,
    low_ref,
    high_ref,
    qd_ref,
    dq_ref,
    to_low,
    to_high,
    in_sems,
    out_sem,
    kn_own,
    knt_own,
    vv_own,
    kn_l,
    knt_l,
    vv_l,
    kn_h,
    knt_h,
    vv_h,
    q_side,
    d_side,
    qn,
    dd,
    chance_own,
    score_own,
    chance_l,
    chance_h,
    score_l,
    score_h,
    gains_ref,
    q_inverse,
):
    arrivals = []
    for col in range(COLS):
        pairs = ((kv_hbm, kv_ref), (low_hbm, low_ref), (high_hbm, high_ref), (qd_hbm, qd_ref))
        copies = [
            pltpu.make_async_copy(source.at[:, :, col], target.at[:, :, col], in_sems.at[col])
            for source, target in pairs
        ]
        for copy in copies:
            copy.start()
        arrivals.append(copies)
    departures = []

    def send(source, target):
        copy = pltpu.make_async_copy(source, target, out_sem)
        copy.start()
        departures.append(copy)

    q_gain = q_gain_ref[...]
    k_gain = k_gain_ref[...]
    def prepare(col):
        for copy in arrivals[col]:
            copy.wait()
        for source, frames, kn, knt, vv in (
            (kv_ref, 2, kn_own, knt_own, vv_own),
            (low_ref, 1, kn_l, knt_l, vv_l),
            (high_ref, 1, kn_h, knt_h, vv_h),
        ):
            for frame in range(frames):
                for row in range(2):
                    raw = source[frame, row, col, 0].astype(F32)
                    normed = (raw * inverse_rms(raw) * k_gain).astype(BF16)
                    for part in range(2):
                        at = ((2 * col + part) * frames + frame) * PAIR + row * TILE
                        kn[at : at + TILE] = normed[part * TILE : (part + 1) * TILE]
                        vv[at : at + TILE] = source[frame, row, col, 1, part * TILE : (part + 1) * TILE]
            for block in range(2 * col * frames, 2 * (col + 1) * frames):
                rows = slice(block * PAIR, (block + 1) * PAIR)
                knt[:, rows] = kn[rows].T
        for frame in range(2):
            for row in range(2):
                raw = qd_ref[frame, row, col, 0].astype(F32)
                inverse = jnp.broadcast_to(inverse_rms(raw), raw.shape)
                normed = (raw * inverse * q_gain).astype(BF16)
                for part in range(2):
                    place = slice(part * TILE, (part + 1) * TILE)
                    at = ((2 * col + part) * 2 + frame) * PAIR + row * TILE
                    q_inverse[at : at + TILE] = inverse[place]
                    qn[at : at + TILE] = normed[place]
                    dd[at : at + TILE] = qd_ref[frame, row, col, 1, place]
                    at = (2 * col + part) * PAIR + row * TILE
                    q_side[frame, at : at + TILE] = normed[place]
                    d_side[frame, at : at + TILE] = qd_ref[frame, row, col, 1, place]

    gains_ref[...] = jnp.zeros_like(gains_ref)
    sources = (
        (kn_own, knt_own, vv_own, chance_own, score_own, 2, 0, 2 * PAIR, None),
        (kn_l, knt_l, vv_l, chance_l, score_l, 1, 0, PAIR, flags_ref[0].astype(F32)),
        (kn_h, knt_h, vv_h, chance_h, score_h, 1, PAIR, PAIR, flags_ref[1].astype(F32)),
    )

    def first_half(w, before, count):
        q_rows = pl.ds(w * (2 * PAIR), 2 * PAIR)
        q_tile = qn[q_rows]
        d_tile = dd[q_rows]
        weights, weight_grads, sums = [], [], []
        for kn, _, vv, _, _, frames, first, width, valid in sources:
            rows = pl.ds((w - before) * (frames * PAIR), count * frames * PAIR)
            queries = slice(first, first + width)
            weight = jnp.exp2(nt(kn[rows], q_tile[queries]) * SCALE_LOG2E)
            if valid is not None:
                weight = weight * valid
            weights.append(weight)
            sums.append(jnp.sum(weight, axis=0, keepdims=True))
            weight_grads.append(nt(vv[rows], d_tile[queries]))
        return q_tile, d_tile, weights, weight_grads, sums

    def second_half(w, before, count, q_tile, d_tile, weights, weight_grads, sums):
        reciprocal = 1.0 / spread(sums)
        dots = []
        for number, (_, _, _, store, _, frames, first, width, _) in enumerate(sources):
            chance = weights[number] * reciprocal[:, first : first + width]
            rounded = chance.astype(BF16)
            dots.append(jnp.sum(rounded.astype(F32) * weight_grads[number], axis=0, keepdims=True))
            for step in range(count):
                place = (1 - (step - before)) * width
                store[w - before + step, :, place : place + width] = rounded[
                    step * frames * PAIR : (step + 1) * frames * PAIR
                ]
        row_dot = spread(dots)
        grads = []
        for number, (_, knt, _, _, store, frames, first, width, _) in enumerate(sources):
            chance = weights[number] * reciprocal[:, first : first + width]
            score = chance * (weight_grads[number] - row_dot[:, first : first + width])
            score = score.astype(BF16)
            for step in range(count):
                place = (1 - (step - before)) * width
                store[w - before + step, :, place : place + width] = score[
                    step * frames * PAIR : (step + 1) * frames * PAIR
                ]
            lanes = pl.ds((w - before) * (frames * PAIR), count * frames * PAIR)
            grads.append(nn(knt[:, lanes], score))
        grad = spread(grads).T * SCALE
        col = w // 2
        place = pl.ds((w % 2) * TILE, TILE)
        for frame in range(2):
            for row in range(2):
                raw = qd_ref[frame, row, col, 0, place].astype(F32)
                at = (2 * w + frame) * PAIR + row * TILE
                inverse = q_inverse[at : at + TILE]
                part = grad[frame * PAIR + row * TILE : frame * PAIR + (row + 1) * TILE]
                gains_ref[0:8] += jnp.sum((part * raw * inverse).reshape(-1, 8, HD), axis=0)
                gains_ref[8:16] += jnp.sum((part * qn[at : at + TILE].astype(F32)).reshape(-1, 8, HD), axis=0)
                dq_ref[frame, row, col, place] = norm_back(raw, inverse, q_gain, part).astype(BF16)
        if w % 2:
            send(dq_ref.at[:, :, col, :PAIR], dq_hbm.at[:, :, col, :PAIR])

    sides = ((chance_l, score_l, to_low, to_low_hbm), (chance_h, score_h, to_high, to_high_hbm))

    def key_column(w):
        for frame, (chance, score, out_ref, out_hbm) in enumerate(sides):
            key_grad, value_grad = key_sums(chance, score, q_side.at[frame], d_side.at[frame], w, PAIR)
            out_ref[w, 0] = key_grad.astype(BF16)
            out_ref[w, 1] = value_grad.astype(BF16)
            send(out_ref.at[w], out_hbm.at[w])
        send(chance_own.at[w], chance_hbm.at[w])
        send(score_own.at[w], score_hbm.at[w])

    def extent(w):
        return w, min(w, 1), 2 if w in (0, WIDE - 1) else 3

    prepare(0)
    held = first_half(*extent(0))
    for w in range(WIDE):
        if w % 2 == 0 and w // 2 + 1 < COLS:
            prepare(w // 2 + 1)
            if w // 2 + 2 == COLS:
                send(qn, qn_hbm)
                send(dd, dd_hbm)
        following = first_half(*extent(w + 1)) if w + 1 < WIDE else None
        second_half(*extent(w), *held)
        held = following
        if w > 0:
            key_column(w - 1)
    key_column(WIDE - 1)


    q_sum = jnp.sum(gains_ref[0:8], axis=0, keepdims=True)
    k_sum = jnp.sum(gains_ref[8:16], axis=0, keepdims=True) / k_gain
    lines = []
    for line in (q_sum, k_sum):
        line = jnp.where(flags_ref[2] > 0, line, 0.0)
        for _ in range(3):
            rounded = line.astype(BF16).astype(F32)
            lines.append(rounded)
            line = line - rounded
    lines.append(jnp.zeros((EXTRA - 6, HD), F32))
    block = jnp.concatenate(lines, axis=0).astype(BF16)
    dq_ref[:, :, :, PAIR:] = jnp.broadcast_to(block, (2, 2, COLS, EXTRA, HD))
    send(dq_ref.at[:, :, :, PAIR:], dq_hbm.at[:, :, :, PAIR:])
    for copy in departures:
        copy.wait()


def grid_of(array):
    return array.reshape((-1, 2, COLS) + array.shape[1:])


def attention(flags, kv, low, high, qd, q_gain, k_gain):
    own, halo = WIDE * 2 * PAIR, WIDE * PAIR
    arrays = [grid_of(array) for array in (kv, low, high, qd)]
    side = ((WIDE, 2, PAIR, HD), BF16)
    columns = ((WIDE, 2 * PAIR, 6 * PAIR), BF16)
    queries = ((own, HD), BF16)
    outs = [((2, 2, COLS, PAIR + EXTRA, HD), BF16), side, side, queries, queries, columns, columns]
    scratch = [pltpu.VMEM(array.shape, BF16) for array in arrays]
    scratch += [pltpu.VMEM(*out) for out in outs[:3]]
    scratch += [pltpu.SemaphoreType.DMA((COLS,)), pltpu.SemaphoreType.DMA]
    for rows in (own, halo, halo):
        scratch += [pltpu.VMEM((rows, HD), BF16), pltpu.VMEM((HD, rows), BF16), pltpu.VMEM((rows, HD), BF16)]
    scratch += [pltpu.VMEM((2, halo, HD), BF16)] * 2 + [pltpu.VMEM(*out) for out in outs[3:]]
    scratch += [pltpu.VMEM((WIDE, PAIR, 3 * PAIR), BF16)] * 4 + [pltpu.VMEM((16, HD), F32)]
    scratch += [pltpu.VMEM((own, HD), F32)]
    dq, *others = pl.pallas_call(
        attention_kernel,
        in_specs=[pl.BlockSpec(memory_space=pltpu.SMEM)]
        + [pl.BlockSpec(memory_space=pl.ANY)] * 4
        + [pl.BlockSpec(memory_space=pltpu.VMEM)] * 2,
        out_specs=[pl.BlockSpec(memory_space=pl.ANY)] * len(outs),
        out_shape=[pltpu.HBM(*out) for out in outs],
        scratch_shapes=scratch,
        name="attention",
        cost_estimate=pl.CostEstimate(
            flops=5 * 66 * PAIR * PAIR * PAIR * 2, bytes_accessed=8 << 20, transcendentals=0
        ),
        compiler_params=pltpu.CompilerParams(vmem_limit_bytes=ATTENTION_LIMIT),
    )(flags, *arrays, q_gain, k_gain)
    return dq.reshape(GROUP, PAIR + EXTRA, HD), *others


def own_kernel(qn_hbm, dd_hbm, chance_hbm, score_hbm, own_hbm, qn, dd, chance, score, own_ref, sems, out_sem):
    arrivals = []
    for w in range(WIDE):
        pairs = [(chance_hbm.at[w], chance.at[w]), (score_hbm.at[w], score.at[w])]
        if w == 0:
            pairs = [(qn_hbm, qn), (dd_hbm, dd)] + pairs
        copies = [pltpu.make_async_copy(source, target, sems.at[w]) for source, target in pairs]
        for copy in copies:
            copy.start()
        arrivals.append(copies)
    departures = []
    for w in range(WIDE):
        for copy in arrivals[w]:
            copy.wait()
        key_grad, value_grad = key_sums(chance, score, qn, dd, w, 2 * PAIR)
        own_ref[w, 0] = key_grad.astype(BF16)
        own_ref[w, 1] = value_grad.astype(BF16)
        copy = pltpu.make_async_copy(own_ref.at[w], own_hbm.at[w], out_sem)
        copy.start()
        departures.append(copy)
    for copy in departures:
        copy.wait()


def own_sums(*arguments):
    out = ((WIDE, 2, 2 * PAIR, HD), BF16)
    return pl.pallas_call(
        own_kernel,
        in_specs=[pl.BlockSpec(memory_space=pl.ANY)] * 4,
        out_specs=pl.BlockSpec(memory_space=pl.ANY),
        out_shape=pltpu.HBM(*out),
        scratch_shapes=[pltpu.VMEM(array.shape, array.dtype) for array in arguments]
        + [pltpu.VMEM(*out), pltpu.SemaphoreType.DMA((WIDE,)), pltpu.SemaphoreType.DMA],
        name="own_sums",
        cost_estimate=pl.CostEstimate(
            flops=2 * 44 * PAIR * PAIR * PAIR * 2, bytes_accessed=8 << 20, transcendentals=0
        ),
        compiler_params=pltpu.CompilerParams(vmem_limit_bytes=LIMIT),
    )(*arguments)


def finish_kernel(frame, kv_ref, own_ref, halo_ref, k_gain_ref, out_hbm, out_ref, sem):
    rows = slice(frame * PAIR, (frame + 1) * PAIR)
    k_gain = k_gain_ref[...]
    departures = []
    for col in range(COLS):
        for part in range(2):
            w = 2 * col + part
            place = slice(part * TILE, (part + 1) * TILE)
            raw = raw_column(kv_ref, w, frame, col)
            key_grad = own_ref[w, 0, rows].astype(F32) + halo_ref[w, 0].astype(F32)
            value_grad = (own_ref[w, 1, rows].astype(F32) + halo_ref[w, 1].astype(F32)).astype(BF16)
            key_grad = norm_back(raw, inverse_rms(raw), k_gain, key_grad).astype(BF16)
            for row in range(2):
                out_ref[row, col, 0, place] = key_grad[row * TILE : (row + 1) * TILE]
                out_ref[row, col, 1, place] = value_grad[row * TILE : (row + 1) * TILE]
        copy = pltpu.make_async_copy(out_ref.at[:, col], out_hbm.at[frame, :, col], sem)
        copy.start()
        departures.append(copy)
    for copy in departures:
        copy.wait()


def second_finish_kernel(kv_ref, own_ref, halo_ref, k_gain_ref, first_hbm, out_hbm, out_ref, sem):
    finish_kernel(1, kv_ref, own_ref, halo_ref, k_gain_ref, out_hbm, out_ref, sem)


def finish(frame, kv, own, halo, k_gain, first=None):
    half = (2, COLS, 2, PAIR, HD)
    arguments = [grid_of(kv), own, halo, k_gain]
    in_specs = [pl.BlockSpec(memory_space=pltpu.VMEM)] * 4
    aliases = {}
    if frame:
        arguments.append(first)
        in_specs.append(pl.BlockSpec(memory_space=pl.ANY))
        aliases = {4: 0}
    return pl.pallas_call(
        second_finish_kernel if frame else functools.partial(finish_kernel, 0),
        in_specs=in_specs,
        out_specs=pl.BlockSpec(memory_space=pl.ANY),
        out_shape=pltpu.HBM((2,) + half, BF16),
        scratch_shapes=[pltpu.VMEM(half, BF16), pltpu.SemaphoreType.DMA],
        input_output_aliases=aliases,
        name="finish_high" if frame else "finish_low",
        compiler_params=pltpu.CompilerParams(vmem_limit_bytes=SMALL),
    )(*arguments)


def unpack_query_kernel(in_ref, out_ref, lines_ref):
    for head in range(HEADS):
        out_ref[0, :, head * HD : (head + 1) * HD] = in_ref[head, :PAIR]
    total = in_ref[0, PAIR:].astype(F32)
    for index in range(1, GROUP):
        total = total + in_ref[index, PAIR:].astype(F32)
    sums = [jnp.sum(total[first : first + 3], axis=0, keepdims=True) for first in (0, 3)]
    lines_ref[...] = jnp.concatenate(sums + [jnp.zeros((6, HD), F32)], axis=0)


def unpack_query(arrived):
    tokens = jax.ShapeDtypeStruct((1, PAIR, HEADS * HD), BF16)
    return pl.pallas_call(
        unpack_query_kernel,
        out_shape=[tokens, jax.ShapeDtypeStruct((8, HD), F32)],
        name="unpack_query",
        compiler_params=pltpu.CompilerParams(vmem_limit_bytes=SMALL),
    )(arrived)


def unpack_kernel(in_ref, key_ref, value_ref, sem):
    copies = []
    for head in range(HEADS):
        lanes = pl.ds(head * HD, HD)
        for number, target in enumerate((key_ref, value_ref)):
            copies.append(pltpu.make_async_copy(in_ref.at[head, number], target.at[0, :, lanes], sem))
    for copy in copies:
        copy.start()
    for copy in copies:
        copy.wait()


def unpack(arrived):
    out = pltpu.HBM((1, PAIR, HEADS * HD), BF16)
    return pl.pallas_call(
        unpack_kernel,
        in_specs=[pl.BlockSpec(memory_space=pltpu.VMEM)],
        out_specs=[pl.BlockSpec(memory_space=pl.ANY)] * 2,
        out_shape=[out, out],
        scratch_shapes=[pltpu.SemaphoreType.DMA],
        name="unpack",
        compiler_params=pltpu.CompilerParams(vmem_limit_bytes=SMALL),
    )(arrived)


def swap(array):
    return lax.all_to_all(array, "g", 0, 0)


def sum_over(lines, axis, steps):
    count = lax.axis_size(axis)
    total = lines
    for step in steps:
        total = total + lax.ppermute(lines, axis, [(source, source ^ step) for source in range(count)])
    return total


def on_device(blocks, q_raw, k_raw, values, d_out, q_gain, k_gain):
    block = lax.axis_index("x")
    member = lax.axis_index("g")
    flags = jnp.stack([block > 0, block < blocks - 1, member < HEADS]).astype(jnp.int32)
    up = [(source, source + 1) for source in range(blocks - 1)]
    down = [(source + 1, source) for source in range(blocks - 1)]
    q_line = q_gain.reshape(1, HD)
    k_line = k_gain.reshape(1, HD)

    kv = swap(pack(k_raw, values))
    low = lax.ppermute(kv[HALF:], "x", up)
    high = lax.ppermute(kv[:HALF], "x", down)
    qd = swap(pack(q_raw, d_out))
    dq, to_low, to_high, *stored = attention(flags, kv, low, high, qd, q_line, k_line)
    arrived = swap(dq)
    from_low = lax.ppermute(to_high, "x", up)
    from_high = lax.ppermute(to_low, "x", down)
    own = own_sums(*stored)
    q_grad, lines = unpack_query(arrived)
    grads = finish(0, kv, own, from_low, k_line)
    grads = finish(1, kv, own, from_high, k_line, grads).reshape(GROUP, 2, PAIR, HD)
    k_grad, v_grad = unpack(swap(grads))
    lines = sum_over(lines, "dp", (1, 2, 3))
    lines = sum_over(lines, "x", (1, 2, 3))
    return (q_grad, k_grad, v_grad, lines[0], lines[1])


def solution(mesh):
    videos, seq = mesh.devices.shape
    blocks = seq // GROUP
    split = Mesh(mesh.devices.reshape(videos, blocks, GROUP), ("dp", "x", "g"))
    tokens = P("dp", ("x", "g"), None)
    return jax.shard_map(
        functools.partial(on_device, blocks),
        mesh=split,
        in_specs=(tokens, tokens, tokens, tokens, P(), P()),
        out_specs=(tokens, tokens, tokens, P(), P()),
        check_vma=False,
    )
```

```python
import functools

import jax
import jax.numpy as jnp
from jax import lax
from jax.experimental import pallas as pl
from jax.experimental.pallas import tpu as pltpu
from jax.sharding import Mesh
from jax.sharding import PartitionSpec as P

HEADS = 12
HD = 128
TILE = 64
PAIR = 2 * TILE
GROUP = 16
HALF = 8
COLS = 4
EXTRA = 16
WIDE = 8
EPSILON = 1e-06
SCALE = HD ** (-0.5)
SCALE_LOG2E = SCALE * 1.4426950408889634
F32 = jnp.float32
BF16 = jnp.bfloat16
LIMIT = 60 * 1024 * 1024
SMALL = 8 * 1024 * 1024
ATTENTION_LIMIT = 36 * 1024 * 1024


def nt(left, right):
    return lax.dot_general(left, right, (((1,), (1,)), ((), ())), preferred_element_type=F32)


def nn(left, right):
    return lax.dot_general(left, right, (((1,), (0,)), ((), ())), preferred_element_type=F32)


def inverse_rms(inputs):
    return lax.rsqrt(jnp.mean(inputs * inputs, axis=-1, keepdims=True) + EPSILON)


def norm_back(inputs, inverse, gain, cotangent):
    scaled = cotangent * gain
    mean = jnp.mean(inputs * scaled, axis=-1, keepdims=True)
    return inverse * scaled - inputs * (inverse * inverse * inverse * mean)


def pack_kernel(first_ref, second_ref, out_ref, sem):
    copies = []
    for head in range(HEADS):
        lanes = pl.ds(head * HD, HD)
        for number, source in enumerate((first_ref, second_ref)):
            copies.append(pltpu.make_async_copy(source.at[0, :, lanes], out_ref.at[head, number], sem))
    for copy in copies:
        copy.start()
    for head in range(HEADS, GROUP):
        out_ref[head] = jnp.zeros(out_ref.shape[1:], out_ref.dtype)
    for copy in copies:
        copy.wait()


def pack(first, second):
    return pl.pallas_call(
        pack_kernel,
        in_specs=[pl.BlockSpec(memory_space=pl.ANY)] * 2,
        out_specs=pl.BlockSpec(memory_space=pltpu.VMEM),
        out_shape=jax.ShapeDtypeStruct((GROUP, 2, PAIR, HD), BF16),
        scratch_shapes=[pltpu.SemaphoreType.DMA],
        name="pack",
        compiler_params=pltpu.CompilerParams(vmem_limit_bytes=LIMIT),
    )(first, second)


def spread(parts):
    return parts[0] + jnp.concatenate(parts[1:], axis=1)


def raw_column(source, w, frame, col):
    place = slice((w % 2) * TILE, (w % 2 + 1) * TILE)
    rows = [source[frame, row, col, 0, place] for row in range(2)]
    return jnp.concatenate(rows, axis=0).astype(F32)


def key_sums(chance, score, queries, cotangents, w, width):
    first, last = max(w - 1, 0), min(w + 1, WIDE - 1)
    lanes = slice((first - w + 1) * width, (last - w + 2) * width)
    rows = slice(first * width, (last + 1) * width)
    value_grad = nn(chance[w, :, lanes], cotangents[rows])
    key_grad = nn(score[w, :, lanes], queries[rows]) * SCALE
    return key_grad, value_grad


def attention_kernel(
    flags_ref,
    kv_hbm,
    low_hbm,
    high_hbm,
    qd_hbm,
    both_gains_hbm,
    dq_hbm,
    to_low_hbm,
    to_high_hbm,
    qn_hbm,
    dd_hbm,
    stats_hbm,
    same_gains_hbm,
    kv_ref,
    low_ref,
    high_ref,
    qd_ref,
    dq_ref,
    to_low,
    to_high,
    in_sems,
    out_sem,
    kn_own,
    knt_own,
    vv_own,
    kn_l,
    knt_l,
    vv_l,
    kn_h,
    knt_h,
    vv_h,
    q_side,
    d_side,
    qn,
    dd,
    stats,
    chance_l,
    chance_h,
    score_l,
    score_h,
    gains_ref,
    q_inverse,
    both_gains,
    gain_sem,
):
    gain_copy = pltpu.make_async_copy(both_gains_hbm, both_gains, gain_sem)
    gain_copy.start()
    arrivals = []
    for col in range(COLS):
        pairs = ((kv_hbm, kv_ref), (low_hbm, low_ref), (high_hbm, high_ref), (qd_hbm, qd_ref))
        copies = [
            pltpu.make_async_copy(source.at[:, :, col], target.at[:, :, col], in_sems.at[col])
            for source, target in pairs
        ]
        for copy in copies:
            copy.start()
        arrivals.append(copies)
    departures = []

    def send(source, target):
        copy = pltpu.make_async_copy(source, target, out_sem)
        copy.start()
        departures.append(copy)

    gain_copy.wait()
    q_gain = both_gains[0:1]
    k_gain = both_gains[1:2]
    def prepare(col):
        for copy in arrivals[col]:
            copy.wait()
        for source, frames, kn, knt, vv in (
            (kv_ref, 2, kn_own, knt_own, vv_own),
            (low_ref, 1, kn_l, knt_l, vv_l),
            (high_ref, 1, kn_h, knt_h, vv_h),
        ):
            for frame in range(frames):
                for row in range(2):
                    raw = source[frame, row, col, 0].astype(F32)
                    normed = (raw * inverse_rms(raw) * k_gain).astype(BF16)
                    for part in range(2):
                        at = ((2 * col + part) * frames + frame) * PAIR + row * TILE
                        kn[at : at + TILE] = normed[part * TILE : (part + 1) * TILE]
                        vv[at : at + TILE] = source[frame, row, col, 1, part * TILE : (part + 1) * TILE]
            for block in range(2 * col * frames, 2 * (col + 1) * frames):
                rows = slice(block * PAIR, (block + 1) * PAIR)
                knt[:, rows] = kn[rows].T
        for frame in range(2):
            for row in range(2):
                raw = qd_ref[frame, row, col, 0].astype(F32)
                inverse = jnp.broadcast_to(inverse_rms(raw), raw.shape)
                normed = (raw * inverse * q_gain).astype(BF16)
                for part in range(2):
                    place = slice(part * TILE, (part + 1) * TILE)
                    at = ((2 * col + part) * 2 + frame) * PAIR + row * TILE
                    q_inverse[at : at + TILE] = inverse[place]
                    qn[at : at + TILE] = normed[place]
                    dd[at : at + TILE] = qd_ref[frame, row, col, 1, place]
                    at = (2 * col + part) * PAIR + row * TILE
                    q_side[frame, at : at + TILE] = normed[place]
                    d_side[frame, at : at + TILE] = qd_ref[frame, row, col, 1, place]

    gains_ref[...] = jnp.zeros_like(gains_ref)
    stats[...] = jnp.zeros_like(stats)
    sources = (
        (kn_own, knt_own, vv_own, None, None, 2, 0, 2 * PAIR, None),
        (kn_l, knt_l, vv_l, chance_l, score_l, 1, 0, PAIR, flags_ref[0].astype(F32)),
        (kn_h, knt_h, vv_h, chance_h, score_h, 1, PAIR, PAIR, flags_ref[1].astype(F32)),
    )

    def first_half(w, before, count):
        q_rows = pl.ds(w * (2 * PAIR), 2 * PAIR)
        q_tile = qn[q_rows]
        d_tile = dd[q_rows]
        weights, weight_grads, sums = [], [], []
        for kn, _, vv, _, _, frames, first, width, valid in sources:
            rows = pl.ds((w - before) * (frames * PAIR), count * frames * PAIR)
            queries = slice(first, first + width)
            weight = jnp.exp2(nt(kn[rows], q_tile[queries]) * SCALE_LOG2E)
            if valid is not None:
                weight = weight * valid
            weights.append(weight)
            sums.append(jnp.sum(weight, axis=0, keepdims=True))
            weight_grads.append(nt(vv[rows], d_tile[queries]))
        return q_tile, d_tile, weights, weight_grads, sums

    def second_half(w, before, count, q_tile, d_tile, weights, weight_grads, sums):
        reciprocal = 1.0 / spread(sums)
        dots = []
        for number, (_, _, _, store, _, frames, first, width, _) in enumerate(sources):
            chance = weights[number] * reciprocal[:, first : first + width]
            rounded = chance.astype(BF16)
            dots.append(jnp.sum(rounded.astype(F32) * weight_grads[number], axis=0, keepdims=True))
            for step in range(count if store is not None else 0):
                place = (1 - (step - before)) * width
                store[w - before + step, :, place : place + width] = rounded[
                    step * frames * PAIR : (step + 1) * frames * PAIR
                ]
        row_dot = spread(dots)
        stats[w, 0:1] = reciprocal
        stats[w, 1:2] = row_dot
        grads = []
        for number, (_, knt, _, _, store, frames, first, width, _) in enumerate(sources):
            chance = weights[number] * reciprocal[:, first : first + width]
            score = chance * (weight_grads[number] - row_dot[:, first : first + width])
            score = score.astype(BF16)
            for step in range(count if store is not None else 0):
                place = (1 - (step - before)) * width
                store[w - before + step, :, place : place + width] = score[
                    step * frames * PAIR : (step + 1) * frames * PAIR
                ]
            lanes = pl.ds((w - before) * (frames * PAIR), count * frames * PAIR)
            grads.append(nn(knt[:, lanes], score))
        grad = spread(grads).T * SCALE
        col = w // 2
        place = pl.ds((w % 2) * TILE, TILE)
        for frame in range(2):
            for row in range(2):
                raw = qd_ref[frame, row, col, 0, place].astype(F32)
                at = (2 * w + frame) * PAIR + row * TILE
                inverse = q_inverse[at : at + TILE]
                part = grad[frame * PAIR + row * TILE : frame * PAIR + (row + 1) * TILE]
                gains_ref[0:8] += jnp.sum((part * raw * inverse).reshape(-1, 8, HD), axis=0)
                gains_ref[8:16] += jnp.sum((part * qn[at : at + TILE].astype(F32)).reshape(-1, 8, HD), axis=0)
                dq_ref[frame, row, col, place] = norm_back(raw, inverse, q_gain, part).astype(BF16)
        if w % 2:
            send(dq_ref.at[:, :, col, :PAIR], dq_hbm.at[:, :, col, :PAIR])

    sides = ((chance_l, score_l, to_low, to_low_hbm), (chance_h, score_h, to_high, to_high_hbm))

    def key_column(w):
        for frame, (chance, score, out_ref, out_hbm) in enumerate(sides):
            key_grad, value_grad = key_sums(chance, score, q_side.at[frame], d_side.at[frame], w, PAIR)
            out_ref[w, 0] = key_grad.astype(BF16)
            out_ref[w, 1] = value_grad.astype(BF16)
            send(out_ref.at[w], out_hbm.at[w])

    def extent(w):
        return w, min(w, 1), 2 if w in (0, WIDE - 1) else 3

    prepare(0)
    held = first_half(*extent(0))
    for w in range(WIDE):
        if w % 2 == 0 and w // 2 + 1 < COLS:
            prepare(w // 2 + 1)
            if w // 2 + 2 == COLS:
                send(qn, qn_hbm)
                send(dd, dd_hbm)
        following = first_half(*extent(w + 1)) if w + 1 < WIDE else None
        second_half(*extent(w), *held)
        held = following
        if w > 0:
            key_column(w - 1)
    send(stats, stats_hbm)
    key_column(WIDE - 1)


    q_sum = jnp.sum(gains_ref[0:8], axis=0, keepdims=True)
    k_sum = jnp.sum(gains_ref[8:16], axis=0, keepdims=True) / k_gain
    lines = []
    for line in (q_sum, k_sum):
        line = jnp.where(flags_ref[2] > 0, line, 0.0)
        for _ in range(3):
            rounded = line.astype(BF16).astype(F32)
            lines.append(rounded)
            line = line - rounded
    lines.append(jnp.zeros((EXTRA - 6, HD), F32))
    block = jnp.concatenate(lines, axis=0).astype(BF16)
    dq_ref[:, :, :, PAIR:] = jnp.broadcast_to(block, (2, 2, COLS, EXTRA, HD))
    send(dq_ref.at[:, :, :, PAIR:], dq_hbm.at[:, :, :, PAIR:])
    for copy in departures:
        copy.wait()


def grid_of(array):
    return array.reshape((-1, 2, COLS) + array.shape[1:])


def attention(flags, kv, low, high, qd, gains):
    own, halo = WIDE * 2 * PAIR, WIDE * PAIR
    arrays = [grid_of(array) for array in (kv, low, high, qd)]
    side = ((WIDE, 2, PAIR, HD), BF16)
    stats = ((WIDE, 8, 2 * PAIR), F32)
    queries = ((own, HD), BF16)
    outs = [((2, 2, COLS, PAIR + EXTRA, HD), BF16), side, side, queries, queries, stats, ((8, HD), F32)]
    scratch = [pltpu.VMEM(array.shape, BF16) for array in arrays]
    scratch += [pltpu.VMEM(*out) for out in outs[:3]]
    scratch += [pltpu.SemaphoreType.DMA((COLS,)), pltpu.SemaphoreType.DMA]
    for rows in (own, halo, halo):
        scratch += [pltpu.VMEM((rows, HD), BF16), pltpu.VMEM((HD, rows), BF16), pltpu.VMEM((rows, HD), BF16)]
    scratch += [pltpu.VMEM((2, halo, HD), BF16)] * 2 + [pltpu.VMEM(*out) for out in outs[3:6]]
    scratch += [pltpu.VMEM((WIDE, PAIR, 3 * PAIR), BF16)] * 4 + [pltpu.VMEM((16, HD), F32)]
    scratch += [pltpu.VMEM((own, HD), F32)] + [pltpu.VMEM((8, HD), F32)] + [pltpu.SemaphoreType.DMA]
    dq, *others, _ = pl.pallas_call(
        attention_kernel,
        in_specs=[pl.BlockSpec(memory_space=pltpu.SMEM)]
        + [pl.BlockSpec(memory_space=pl.ANY)] * 5,
        out_specs=[pl.BlockSpec(memory_space=pl.ANY)] * len(outs),
        out_shape=[pltpu.HBM(*out) for out in outs],
        scratch_shapes=scratch,
        input_output_aliases={5: len(outs) - 1},
        name="attention",
        cost_estimate=pl.CostEstimate(
            flops=5 * 66 * PAIR * PAIR * PAIR * 2, bytes_accessed=8 << 20, transcendentals=0
        ),
        compiler_params=pltpu.CompilerParams(vmem_limit_bytes=ATTENTION_LIMIT),
    )(flags, *arrays, gains)
    return dq.reshape(GROUP, PAIR + EXTRA, HD), *others


def own_kernel(
    kv_hbm,
    qn_hbm,
    dd_hbm,
    stats_hbm,
    k_gain_ref,
    own_hbm,
    kv_ref,
    qn,
    dd,
    stats,
    own_ref,
    kn,
    vv,
    chance_own,
    score_own,
    query_sem,
    in_sems,
    out_sem,
):
    queries = [
        pltpu.make_async_copy(source, target, query_sem)
        for source, target in ((qn_hbm, qn), (dd_hbm, dd), (stats_hbm, stats))
    ]
    arrivals = [
        pltpu.make_async_copy(kv_hbm.at[:, :, col], kv_ref.at[:, :, col], in_sems.at[col]) for col in range(COLS)
    ]
    for copy in arrivals[:1] + queries + arrivals[1:]:
        copy.start()
    k_gain = k_gain_ref[...]

    def prepare(col):
        arrivals[col].wait()
        for frame in range(2):
            for row in range(2):
                raw = kv_ref[frame, row, col, 0].astype(F32)
                normed = (raw * inverse_rms(raw) * k_gain).astype(BF16)
                for part in range(2):
                    place = slice(part * TILE, (part + 1) * TILE)
                    at = ((2 * col + part) * 2 + frame) * PAIR + row * TILE
                    kn[at : at + TILE] = normed[place]
                    vv[at : at + TILE] = kv_ref[frame, row, col, 1, place]

    def products(w):
        first, last = max(w - 1, 0), min(w + 1, WIDE - 1)
        rows = slice(first * 2 * PAIR, (last + 1) * 2 * PAIR)
        q_rows = slice(w * 2 * PAIR, (w + 1) * 2 * PAIR)
        weights = jnp.exp2(nt(kn[rows], qn[q_rows]) * SCALE_LOG2E)
        return first, last, weights, nt(vv[rows], dd[q_rows])

    def scores(w, first, last, weights, weight_grads):
        chance = weights * stats[w, 0:1]
        rounded = chance.astype(BF16)
        score = (chance * (weight_grads - stats[w, 1:2])).astype(BF16)
        for column in range(first, last + 1):
            part = slice((column - first) * 2 * PAIR, (column - first + 1) * 2 * PAIR)
            place = (1 - (column - w)) * 2 * PAIR
            chance_own[column, :, place : place + 2 * PAIR] = rounded[part]
            score_own[column, :, place : place + 2 * PAIR] = score[part]

    departures = []

    def key_column(w):
        key_grad, value_grad = key_sums(chance_own, score_own, qn, dd, w, 2 * PAIR)
        own_ref[w, 0] = key_grad.astype(BF16)
        own_ref[w, 1] = value_grad.astype(BF16)
        copy = pltpu.make_async_copy(own_ref.at[w], own_hbm.at[w], out_sem)
        copy.start()
        departures.append(copy)

    prepare(0)
    for copy in queries:
        copy.wait()
    held = products(0)
    for w in range(WIDE):
        if w % 2 == 0 and w // 2 + 1 < COLS:
            prepare(w // 2 + 1)
        following = products(w + 1) if w + 1 < WIDE else None
        scores(w, *held)
        held = following
        if w > 0:
            key_column(w - 1)
    key_column(WIDE - 1)
    for copy in departures:
        copy.wait()


def own_sums(kv, qn, dd, stats, k_gain):
    out = ((WIDE, 2, 2 * PAIR, HD), BF16)
    arrays = [grid_of(kv), qn, dd, stats]
    scratch = [pltpu.VMEM(array.shape, array.dtype) for array in arrays] + [pltpu.VMEM(*out)]
    scratch += [pltpu.VMEM(qn.shape, BF16)] * 2 + [pltpu.VMEM((WIDE, 2 * PAIR, 6 * PAIR), BF16)] * 2
    scratch += [pltpu.SemaphoreType.DMA, pltpu.SemaphoreType.DMA((COLS,)), pltpu.SemaphoreType.DMA]
    return pl.pallas_call(
        own_kernel,
        in_specs=[pl.BlockSpec(memory_space=pl.ANY)] * 4 + [pl.BlockSpec(memory_space=pltpu.VMEM)],
        out_specs=pl.BlockSpec(memory_space=pl.ANY),
        out_shape=pltpu.HBM(*out),
        scratch_shapes=scratch,
        name="own_sums",
        cost_estimate=pl.CostEstimate(
            flops=4 * 44 * PAIR * PAIR * PAIR * 2, bytes_accessed=8 << 20, transcendentals=0
        ),
        compiler_params=pltpu.CompilerParams(vmem_limit_bytes=LIMIT),
    )(*arrays, k_gain)


def finish_kernel(frame, kv_ref, own_ref, halo_ref, k_gain_ref, out_hbm, out_ref, sem):
    rows = slice(frame * PAIR, (frame + 1) * PAIR)
    k_gain = k_gain_ref[...]
    departures = []
    for col in range(COLS):
        for part in range(2):
            w = 2 * col + part
            place = slice(part * TILE, (part + 1) * TILE)
            raw = raw_column(kv_ref, w, frame, col)
            key_grad = own_ref[w, 0, rows].astype(F32) + halo_ref[w, 0].astype(F32)
            value_grad = (own_ref[w, 1, rows].astype(F32) + halo_ref[w, 1].astype(F32)).astype(BF16)
            key_grad = norm_back(raw, inverse_rms(raw), k_gain, key_grad).astype(BF16)
            for row in range(2):
                out_ref[row, col, 0, place] = key_grad[row * TILE : (row + 1) * TILE]
                out_ref[row, col, 1, place] = value_grad[row * TILE : (row + 1) * TILE]
        copy = pltpu.make_async_copy(out_ref.at[:, col], out_hbm.at[frame, :, col], sem)
        copy.start()
        departures.append(copy)
    for copy in departures:
        copy.wait()


def second_finish_kernel(kv_ref, own_ref, halo_ref, k_gain_ref, first_hbm, out_hbm, out_ref, sem):
    finish_kernel(1, kv_ref, own_ref, halo_ref, k_gain_ref, out_hbm, out_ref, sem)


def finish(frame, kv, own, halo, k_gain, first=None):
    half = (2, COLS, 2, PAIR, HD)
    arguments = [grid_of(kv), own, halo, k_gain]
    in_specs = [pl.BlockSpec(memory_space=pltpu.VMEM)] * 4
    aliases = {}
    if frame:
        arguments.append(first)
        in_specs.append(pl.BlockSpec(memory_space=pl.ANY))
        aliases = {4: 0}
    return pl.pallas_call(
        second_finish_kernel if frame else functools.partial(finish_kernel, 0),
        in_specs=in_specs,
        out_specs=pl.BlockSpec(memory_space=pl.ANY),
        out_shape=pltpu.HBM((2,) + half, BF16),
        scratch_shapes=[pltpu.VMEM(half, BF16), pltpu.SemaphoreType.DMA],
        input_output_aliases=aliases,
        name="finish_high" if frame else "finish_low",
        compiler_params=pltpu.CompilerParams(vmem_limit_bytes=SMALL),
    )(*arguments)


def unpack_query_kernel(in_ref, out_ref, lines_ref):
    for head in range(HEADS):
        out_ref[0, :, head * HD : (head + 1) * HD] = in_ref[head, :PAIR]
    total = in_ref[0, PAIR:].astype(F32)
    for index in range(1, GROUP):
        total = total + in_ref[index, PAIR:].astype(F32)
    sums = [jnp.sum(total[first : first + 3], axis=0, keepdims=True) for first in (0, 3)]
    lines_ref[...] = jnp.concatenate(sums + [jnp.zeros((6, HD), F32)], axis=0)


def unpack_query(arrived):
    tokens = jax.ShapeDtypeStruct((1, PAIR, HEADS * HD), BF16)
    return pl.pallas_call(
        unpack_query_kernel,
        out_shape=[tokens, jax.ShapeDtypeStruct((8, HD), F32)],
        name="unpack_query",
        compiler_params=pltpu.CompilerParams(vmem_limit_bytes=SMALL),
    )(arrived)


def unpack_kernel(in_ref, key_ref, value_ref, sem):
    copies = []
    for head in range(HEADS):
        lanes = pl.ds(head * HD, HD)
        for number, target in enumerate((key_ref, value_ref)):
            copies.append(pltpu.make_async_copy(in_ref.at[head, number], target.at[0, :, lanes], sem))
    for copy in copies:
        copy.start()
    for copy in copies:
        copy.wait()


def unpack(arrived):
    out = pltpu.HBM((1, PAIR, HEADS * HD), BF16)
    return pl.pallas_call(
        unpack_kernel,
        in_specs=[pl.BlockSpec(memory_space=pltpu.VMEM)],
        out_specs=[pl.BlockSpec(memory_space=pl.ANY)] * 2,
        out_shape=[out, out],
        scratch_shapes=[pltpu.SemaphoreType.DMA],
        name="unpack",
        compiler_params=pltpu.CompilerParams(vmem_limit_bytes=SMALL),
    )(arrived)


def swap(array):
    return lax.all_to_all(array, "g", 0, 0)


def sum_over(lines, axis, steps):
    count = lax.axis_size(axis)
    total = lines
    for step in steps:
        total = total + lax.ppermute(lines, axis, [(source, source ^ step) for source in range(count)])
    return total


def on_device(blocks, q_raw, k_raw, values, d_out, q_gain, k_gain):
    block = lax.axis_index("x")
    member = lax.axis_index("g")
    flags = jnp.stack([block > 0, block < blocks - 1, member < HEADS]).astype(jnp.int32)
    up = [(source, source + 1) for source in range(blocks - 1)]
    down = [(source + 1, source) for source in range(blocks - 1)]
    q_line = q_gain.reshape(1, HD)
    k_line = k_gain.reshape(1, HD)
    gains = jnp.concatenate([q_line, k_line, jnp.ones((6, HD), F32)], axis=0)

    kv = swap(pack(k_raw, values))
    low = lax.ppermute(kv[HALF:], "x", up)
    high = lax.ppermute(kv[:HALF], "x", down)
    qd = swap(pack(q_raw, d_out))
    dq, to_low, to_high, *stored = attention(flags, kv, low, high, qd, gains)
    arrived = swap(dq)
    from_low = lax.ppermute(to_high, "x", up)
    from_high = lax.ppermute(to_low, "x", down)
    own = own_sums(kv, *stored, k_line)
    q_grad, lines = unpack_query(arrived)
    grads = finish(0, kv, own, from_low, k_line)
    grads = finish(1, kv, own, from_high, k_line, grads).reshape(GROUP, 2, PAIR, HD)
    k_grad, v_grad = unpack(swap(grads))
    lines = sum_over(lines, "dp", (1, 2, 3))
    lines = sum_over(lines, "x", (1, 2, 3))
    return (q_grad, k_grad, v_grad, lines[0], lines[1])


def solution(mesh):
    videos, seq = mesh.devices.shape
    blocks = seq // GROUP
    split = Mesh(mesh.devices.reshape(videos, blocks, GROUP), ("dp", "x", "g"))
    tokens = P("dp", ("x", "g"), None)
    return jax.shard_map(
        functools.partial(on_device, blocks),
        mesh=split,
        in_specs=(tokens, tokens, tokens, tokens, P(), P()),
        out_specs=(tokens, tokens, tokens, P(), P()),
        check_vma=False,
    )
```

```python
import functools

import jax
import jax.numpy as jnp
from jax import lax
from jax.experimental import pallas as pl
from jax.experimental.pallas import tpu as pltpu
from jax.sharding import Mesh
from jax.sharding import PartitionSpec as P

HEADS = 12
HD = 128
TILE = 64
PAIR = 2 * TILE
GROUP = 16
HALF = 8
COLS = 4
EXTRA = 16
WIDE = 8
EPSILON = 1e-06
SCALE = HD ** (-0.5)
SCALE_LOG2E = SCALE * 1.4426950408889634
F32 = jnp.float32
BF16 = jnp.bfloat16
LIMIT = 60 * 1024 * 1024
SMALL = 8 * 1024 * 1024
ATTENTION_LIMIT = 36 * 1024 * 1024


def nt(left, right):
    return lax.dot_general(left, right, (((1,), (1,)), ((), ())), preferred_element_type=F32)


def nn(left, right):
    return lax.dot_general(left, right, (((1,), (0,)), ((), ())), preferred_element_type=F32)


def inverse_rms(inputs):
    return lax.rsqrt(jnp.mean(inputs * inputs, axis=-1, keepdims=True) + EPSILON)


def norm_back(inputs, inverse, gain, cotangent):
    scaled = cotangent * gain
    mean = jnp.mean(inputs * scaled, axis=-1, keepdims=True)
    return inverse * scaled - inputs * (inverse * inverse * inverse * mean)


def pack_kernel(first_ref, second_ref, out_ref, sem):
    copies = []
    for head in range(HEADS):
        lanes = pl.ds(head * HD, HD)
        for number, source in enumerate((first_ref, second_ref)):
            copies.append(pltpu.make_async_copy(source.at[0, :, lanes], out_ref.at[head, number], sem))
    for copy in copies:
        copy.start()
    for head in range(HEADS, GROUP):
        out_ref[head] = jnp.zeros(out_ref.shape[1:], out_ref.dtype)
    for copy in copies:
        copy.wait()


def pack(first, second):
    return pl.pallas_call(
        pack_kernel,
        in_specs=[pl.BlockSpec(memory_space=pl.ANY)] * 2,
        out_specs=pl.BlockSpec(memory_space=pltpu.VMEM),
        out_shape=jax.ShapeDtypeStruct((GROUP, 2, PAIR, HD), BF16),
        scratch_shapes=[pltpu.SemaphoreType.DMA],
        name="pack",
        compiler_params=pltpu.CompilerParams(vmem_limit_bytes=LIMIT),
    )(first, second)


def spread(parts):
    return parts[0] + jnp.concatenate(parts[1:], axis=1)


def raw_column(source, w, frame, col):
    place = slice((w % 2) * TILE, (w % 2 + 1) * TILE)
    rows = [source[frame, row, col, 0, place] for row in range(2)]
    return jnp.concatenate(rows, axis=0).astype(F32)


def key_sums(chance, score, queries, cotangents, w, width):
    first, last = max(w - 1, 0), min(w + 1, WIDE - 1)
    lanes = slice((first - w + 1) * width, (last - w + 2) * width)
    rows = slice(first * width, (last + 1) * width)
    value_grad = nn(chance[w, :, lanes], cotangents[rows])
    key_grad = nn(score[w, :, lanes], queries[rows]) * SCALE
    return key_grad, value_grad


def attention_kernel(
    flags_ref,
    kv_hbm,
    low_hbm,
    high_hbm,
    qd_hbm,
    both_gains_hbm,
    dq_hbm,
    to_low_hbm,
    to_high_hbm,
    qn_hbm,
    dd_hbm,
    stats_hbm,
    same_gains_hbm,
    kv_ref,
    low_ref,
    high_ref,
    qd_ref,
    dq_ref,
    to_low,
    to_high,
    in_sems,
    out_sem,
    kn_own,
    knt_own,
    vv_own,
    kn_l,
    knt_l,
    vv_l,
    kn_h,
    knt_h,
    vv_h,
    q_side,
    d_side,
    qn,
    dd,
    stats,
    chance_l,
    chance_h,
    score_l,
    score_h,
    gains_ref,
    q_inverse,
    both_gains,
    gain_sem,
):
    gain_copy = pltpu.make_async_copy(both_gains_hbm, both_gains, gain_sem)
    gain_copy.start()
    arrivals = []
    for col in range(COLS):
        pairs = ((kv_hbm, kv_ref), (low_hbm, low_ref), (high_hbm, high_ref), (qd_hbm, qd_ref))
        copies = [
            pltpu.make_async_copy(source.at[:, :, col], target.at[:, :, col], in_sems.at[col])
            for source, target in pairs
        ]
        for copy in copies:
            copy.start()
        arrivals.append(copies)
    departures = []

    def send(source, target):
        copy = pltpu.make_async_copy(source, target, out_sem)
        copy.start()
        departures.append(copy)

    gain_copy.wait()
    q_gain = both_gains[0:1]
    k_gain = both_gains[1:2]
    def prepare(col):
        for copy in arrivals[col]:
            copy.wait()
        for source, frames, kn, knt, vv in (
            (kv_ref, 2, kn_own, knt_own, vv_own),
            (low_ref, 1, kn_l, knt_l, vv_l),
            (high_ref, 1, kn_h, knt_h, vv_h),
        ):
            for frame in range(frames):
                for row in range(2):
                    raw = source[frame, row, col, 0].astype(F32)
                    normed = (raw * inverse_rms(raw) * k_gain).astype(BF16)
                    for part in range(2):
                        at = ((2 * col + part) * frames + frame) * PAIR + row * TILE
                        kn[at : at + TILE] = normed[part * TILE : (part + 1) * TILE]
                        vv[at : at + TILE] = source[frame, row, col, 1, part * TILE : (part + 1) * TILE]
            for block in range(2 * col * frames, 2 * (col + 1) * frames):
                rows = slice(block * PAIR, (block + 1) * PAIR)
                knt[:, rows] = kn[rows].T
        for frame in range(2):
            for row in range(2):
                raw = qd_ref[frame, row, col, 0].astype(F32)
                inverse = jnp.broadcast_to(inverse_rms(raw), raw.shape)
                normed = (raw * inverse * q_gain).astype(BF16)
                for part in range(2):
                    place = slice(part * TILE, (part + 1) * TILE)
                    at = ((2 * col + part) * 2 + frame) * PAIR + row * TILE
                    q_inverse[at : at + TILE] = inverse[place]
                    qn[at : at + TILE] = normed[place]
                    dd[at : at + TILE] = qd_ref[frame, row, col, 1, place]
                    at = (2 * col + part) * PAIR + row * TILE
                    q_side[frame, at : at + TILE] = normed[place]
                    d_side[frame, at : at + TILE] = qd_ref[frame, row, col, 1, place]

    gains_ref[...] = jnp.zeros_like(gains_ref)
    stats[...] = jnp.zeros_like(stats)
    sources = (
        (kn_own, knt_own, vv_own, None, None, 2, 0, 2 * PAIR, None),
        (kn_l, knt_l, vv_l, chance_l, score_l, 1, 0, PAIR, flags_ref[0].astype(F32)),
        (kn_h, knt_h, vv_h, chance_h, score_h, 1, PAIR, PAIR, flags_ref[1].astype(F32)),
    )

    def first_half(w, before, count):
        q_rows = pl.ds(w * (2 * PAIR), 2 * PAIR)
        q_tile = qn[q_rows]
        d_tile = dd[q_rows]
        weights, weight_grads, sums = [], [], []
        for kn, _, vv, _, _, frames, first, width, valid in sources:
            rows = pl.ds((w - before) * (frames * PAIR), count * frames * PAIR)
            queries = slice(first, first + width)
            weight = jnp.exp2(nt(kn[rows], q_tile[queries]) * SCALE_LOG2E)
            if valid is not None:
                weight = weight * valid
            weights.append(weight)
            sums.append(jnp.sum(weight, axis=0, keepdims=True))
            weight_grads.append(nt(vv[rows], d_tile[queries]))
        return q_tile, d_tile, weights, weight_grads, sums

    def second_half(w, before, count, q_tile, d_tile, weights, weight_grads, sums):
        reciprocal = 1.0 / spread(sums)
        dots = []
        for number, (_, _, _, store, _, frames, first, width, _) in enumerate(sources):
            chance = weights[number] * reciprocal[:, first : first + width]
            rounded = chance.astype(BF16)
            dots.append(jnp.sum(rounded.astype(F32) * weight_grads[number], axis=0, keepdims=True))
            for step in range(count if store is not None else 0):
                place = (1 - (step - before)) * width
                store[w - before + step, :, place : place + width] = rounded[
                    step * frames * PAIR : (step + 1) * frames * PAIR
                ]
        row_dot = spread(dots)
        stats[w, 0:1] = reciprocal
        stats[w, 1:2] = row_dot
        grads = []
        for number, (_, knt, _, _, store, frames, first, width, _) in enumerate(sources):
            chance = weights[number] * reciprocal[:, first : first + width]
            score = chance * (weight_grads[number] - row_dot[:, first : first + width])
            score = score.astype(BF16)
            for step in range(count if store is not None else 0):
                place = (1 - (step - before)) * width
                store[w - before + step, :, place : place + width] = score[
                    step * frames * PAIR : (step + 1) * frames * PAIR
                ]
            lanes = pl.ds((w - before) * (frames * PAIR), count * frames * PAIR)
            grads.append(nn(knt[:, lanes], score))
        grad = spread(grads).T * SCALE
        col = w // 2
        place = pl.ds((w % 2) * TILE, TILE)
        for frame in range(2):
            for row in range(2):
                raw = qd_ref[frame, row, col, 0, place].astype(F32)
                at = (2 * w + frame) * PAIR + row * TILE
                inverse = q_inverse[at : at + TILE]
                part = grad[frame * PAIR + row * TILE : frame * PAIR + (row + 1) * TILE]
                gains_ref[0:8] += jnp.sum((part * raw * inverse).reshape(-1, 8, HD), axis=0)
                gains_ref[8:16] += jnp.sum((part * qn[at : at + TILE].astype(F32)).reshape(-1, 8, HD), axis=0)
                dq_ref[frame, row, col, place] = norm_back(raw, inverse, q_gain, part).astype(BF16)
        if w % 2:
            send(dq_ref.at[:, :, col, :PAIR], dq_hbm.at[:, :, col, :PAIR])

    sides = ((chance_l, score_l, to_low, to_low_hbm), (chance_h, score_h, to_high, to_high_hbm))

    def key_column(w):
        for frame, (chance, score, out_ref, out_hbm) in enumerate(sides):
            key_grad, value_grad = key_sums(chance, score, q_side.at[frame], d_side.at[frame], w, PAIR)
            out_ref[w, 0] = key_grad.astype(BF16)
            out_ref[w, 1] = value_grad.astype(BF16)
            send(out_ref.at[w], out_hbm.at[w])

    def extent(w):
        return w, min(w, 1), 2 if w in (0, WIDE - 1) else 3

    prepare(0)
    held = first_half(*extent(0))
    for w in range(WIDE):
        if w % 2 == 0 and w // 2 + 1 < COLS:
            prepare(w // 2 + 1)
            if w // 2 + 2 == COLS:
                send(qn, qn_hbm)
                send(dd, dd_hbm)
        following = first_half(*extent(w + 1)) if w + 1 < WIDE else None
        second_half(*extent(w), *held)
        held = following
        if w > 0:
            key_column(w - 1)
    send(stats, stats_hbm)
    key_column(WIDE - 1)


    q_sum = jnp.sum(gains_ref[0:8], axis=0, keepdims=True)
    k_sum = jnp.sum(gains_ref[8:16], axis=0, keepdims=True) / k_gain
    lines = []
    for line in (q_sum, k_sum):
        line = jnp.where(flags_ref[2] > 0, line, 0.0)
        for _ in range(3):
            rounded = line.astype(BF16).astype(F32)
            lines.append(rounded)
            line = line - rounded
    lines.append(jnp.zeros((EXTRA - 6, HD), F32))
    block = jnp.concatenate(lines, axis=0).astype(BF16)
    dq_ref[:, :, :, PAIR:] = jnp.broadcast_to(block, (2, 2, COLS, EXTRA, HD))
    send(dq_ref.at[:, :, :, PAIR:], dq_hbm.at[:, :, :, PAIR:])
    for copy in departures:
        copy.wait()


def grid_of(array):
    return array.reshape((-1, 2, COLS) + array.shape[1:])


def attention(flags, kv, low, high, qd, gains):
    own, halo = WIDE * 2 * PAIR, WIDE * PAIR
    arrays = [grid_of(array) for array in (kv, low, high, qd)]
    side = ((WIDE, 2, PAIR, HD), BF16)
    stats = ((WIDE, 8, 2 * PAIR), F32)
    queries = ((own, HD), BF16)
    outs = [((2, 2, COLS, PAIR + EXTRA, HD), BF16), side, side, queries, queries, stats, ((8, HD), F32)]
    scratch = [pltpu.VMEM(array.shape, BF16) for array in arrays]
    scratch += [pltpu.VMEM(*out) for out in outs[:3]]
    scratch += [pltpu.SemaphoreType.DMA((COLS,)), pltpu.SemaphoreType.DMA]
    for rows in (own, halo, halo):
        scratch += [pltpu.VMEM((rows, HD), BF16), pltpu.VMEM((HD, rows), BF16), pltpu.VMEM((rows, HD), BF16)]
    scratch += [pltpu.VMEM((2, halo, HD), BF16)] * 2 + [pltpu.VMEM(*out) for out in outs[3:6]]
    scratch += [pltpu.VMEM((WIDE, PAIR, 3 * PAIR), BF16)] * 4 + [pltpu.VMEM((16, HD), F32)]
    scratch += [pltpu.VMEM((own, HD), F32)] + [pltpu.VMEM((8, HD), F32)] + [pltpu.SemaphoreType.DMA]
    dq, *others, _ = pl.pallas_call(
        attention_kernel,
        in_specs=[pl.BlockSpec(memory_space=pltpu.SMEM)]
        + [pl.BlockSpec(memory_space=pl.ANY)] * 5,
        out_specs=[pl.BlockSpec(memory_space=pl.ANY)] * len(outs),
        out_shape=[pltpu.HBM(*out) for out in outs],
        scratch_shapes=scratch,
        input_output_aliases={5: len(outs) - 1},
        name="attention",
        cost_estimate=pl.CostEstimate(
            flops=5 * 66 * PAIR * PAIR * PAIR * 2, bytes_accessed=8 << 20, transcendentals=0
        ),
        compiler_params=pltpu.CompilerParams(vmem_limit_bytes=ATTENTION_LIMIT),
    )(flags, *arrays, gains)
    return dq.reshape(GROUP, PAIR + EXTRA, HD), *others


def own_kernel(
    kv_hbm,
    qn_hbm,
    dd_hbm,
    stats_hbm,
    k_gain_ref,
    own_ref,
    kv_ref,
    qn,
    dd,
    stats,
    kn,
    vv,
    chance_own,
    score_own,
    query_sem,
    in_sems,
):
    queries = [
        pltpu.make_async_copy(source, target, query_sem)
        for source, target in ((qn_hbm, qn), (dd_hbm, dd), (stats_hbm, stats))
    ]
    arrivals = [
        pltpu.make_async_copy(kv_hbm.at[:, :, col], kv_ref.at[:, :, col], in_sems.at[col]) for col in range(COLS)
    ]
    for copy in arrivals[:1] + queries + arrivals[1:]:
        copy.start()
    k_gain = k_gain_ref[...]

    def prepare(col):
        arrivals[col].wait()
        for frame in range(2):
            for row in range(2):
                raw = kv_ref[frame, row, col, 0].astype(F32)
                normed = (raw * inverse_rms(raw) * k_gain).astype(BF16)
                for part in range(2):
                    place = slice(part * TILE, (part + 1) * TILE)
                    at = ((2 * col + part) * 2 + frame) * PAIR + row * TILE
                    kn[at : at + TILE] = normed[place]
                    vv[at : at + TILE] = kv_ref[frame, row, col, 1, place]

    def products(w):
        first, last = max(w - 1, 0), min(w + 1, WIDE - 1)
        rows = slice(first * 2 * PAIR, (last + 1) * 2 * PAIR)
        q_rows = slice(w * 2 * PAIR, (w + 1) * 2 * PAIR)
        weights = jnp.exp2(nt(kn[rows], qn[q_rows]) * SCALE_LOG2E)
        return first, last, weights, nt(vv[rows], dd[q_rows])

    def scores(w, first, last, weights, weight_grads):
        chance = weights * stats[w, 0:1]
        rounded = chance.astype(BF16)
        score = (chance * (weight_grads - stats[w, 1:2])).astype(BF16)
        for column in range(first, last + 1):
            part = slice((column - first) * 2 * PAIR, (column - first + 1) * 2 * PAIR)
            place = (1 - (column - w)) * 2 * PAIR
            chance_own[column, :, place : place + 2 * PAIR] = rounded[part]
            score_own[column, :, place : place + 2 * PAIR] = score[part]

    def key_column(w):
        key_grad, value_grad = key_sums(chance_own, score_own, qn, dd, w, 2 * PAIR)
        own_ref[w, 0] = key_grad.astype(BF16)
        own_ref[w, 1] = value_grad.astype(BF16)

    prepare(0)
    for copy in queries:
        copy.wait()
    held = products(0)
    for w in range(WIDE):
        if w % 2 == 0 and w // 2 + 1 < COLS:
            prepare(w // 2 + 1)
        following = products(w + 1) if w + 1 < WIDE else None
        scores(w, *held)
        held = following
        if w > 0:
            key_column(w - 1)
    key_column(WIDE - 1)


def own_sums(kv, qn, dd, stats, k_gain):
    out = ((WIDE, 2, 2 * PAIR, HD), BF16)
    arrays = [grid_of(kv), qn, dd, stats]
    scratch = [pltpu.VMEM(array.shape, array.dtype) for array in arrays]
    scratch += [pltpu.VMEM(qn.shape, BF16)] * 2 + [pltpu.VMEM((WIDE, 2 * PAIR, 6 * PAIR), BF16)] * 2
    scratch += [pltpu.SemaphoreType.DMA, pltpu.SemaphoreType.DMA((COLS,))]
    return pl.pallas_call(
        own_kernel,
        in_specs=[pl.BlockSpec(memory_space=pl.ANY)] * 4 + [pl.BlockSpec(memory_space=pltpu.VMEM)],
        out_specs=pl.BlockSpec(memory_space=pltpu.VMEM),
        out_shape=jax.ShapeDtypeStruct(*out),
        scratch_shapes=scratch,
        name="own_sums",
        cost_estimate=pl.CostEstimate(
            flops=4 * 44 * PAIR * PAIR * PAIR * 2, bytes_accessed=8 << 20, transcendentals=0
        ),
        compiler_params=pltpu.CompilerParams(vmem_limit_bytes=ATTENTION_LIMIT),
    )(*arrays, k_gain)


def finish_kernel(frame, kv_ref, own_ref, halo_ref, k_gain_ref, out_hbm, out_ref, sem):
    rows = slice(frame * PAIR, (frame + 1) * PAIR)
    k_gain = k_gain_ref[...]
    departures = []
    for col in range(COLS):
        for part in range(2):
            w = 2 * col + part
            place = slice(part * TILE, (part + 1) * TILE)
            raw = raw_column(kv_ref, w, frame, col)
            key_grad = own_ref[w, 0, rows].astype(F32) + halo_ref[w, 0].astype(F32)
            value_grad = (own_ref[w, 1, rows].astype(F32) + halo_ref[w, 1].astype(F32)).astype(BF16)
            key_grad = norm_back(raw, inverse_rms(raw), k_gain, key_grad).astype(BF16)
            for row in range(2):
                out_ref[row, col, 0, place] = key_grad[row * TILE : (row + 1) * TILE]
                out_ref[row, col, 1, place] = value_grad[row * TILE : (row + 1) * TILE]
        copy = pltpu.make_async_copy(out_ref.at[:, col], out_hbm.at[frame, :, col], sem)
        copy.start()
        departures.append(copy)
    for copy in departures:
        copy.wait()


def second_finish_kernel(kv_ref, own_ref, halo_ref, k_gain_ref, first_hbm, out_hbm, out_ref, sem):
    finish_kernel(1, kv_ref, own_ref, halo_ref, k_gain_ref, out_hbm, out_ref, sem)


def finish(frame, kv, own, halo, k_gain, first=None):
    half = (2, COLS, 2, PAIR, HD)
    arguments = [grid_of(kv), own, halo, k_gain]
    in_specs = [pl.BlockSpec(memory_space=pltpu.VMEM)] * 4
    aliases = {}
    if frame:
        arguments.append(first)
        in_specs.append(pl.BlockSpec(memory_space=pl.ANY))
        aliases = {4: 0}
    return pl.pallas_call(
        second_finish_kernel if frame else functools.partial(finish_kernel, 0),
        in_specs=in_specs,
        out_specs=pl.BlockSpec(memory_space=pl.ANY),
        out_shape=pltpu.HBM((2,) + half, BF16),
        scratch_shapes=[pltpu.VMEM(half, BF16), pltpu.SemaphoreType.DMA],
        input_output_aliases=aliases,
        name="finish_high" if frame else "finish_low",
        compiler_params=pltpu.CompilerParams(vmem_limit_bytes=SMALL),
    )(*arguments)


def unpack_query_kernel(in_ref, out_ref, lines_ref):
    for head in range(HEADS):
        out_ref[0, :, head * HD : (head + 1) * HD] = in_ref[head, :PAIR]
    total = in_ref[0, PAIR:].astype(F32)
    for index in range(1, GROUP):
        total = total + in_ref[index, PAIR:].astype(F32)
    sums = [jnp.sum(total[first : first + 3], axis=0, keepdims=True) for first in (0, 3)]
    lines_ref[...] = jnp.concatenate(sums + [jnp.zeros((6, HD), F32)], axis=0)


def unpack_query(arrived):
    tokens = jax.ShapeDtypeStruct((1, PAIR, HEADS * HD), BF16)
    return pl.pallas_call(
        unpack_query_kernel,
        out_shape=[tokens, jax.ShapeDtypeStruct((8, HD), F32)],
        name="unpack_query",
        compiler_params=pltpu.CompilerParams(vmem_limit_bytes=SMALL),
    )(arrived)


def unpack_kernel(in_ref, key_ref, value_ref, sem):
    copies = []
    for head in range(HEADS):
        lanes = pl.ds(head * HD, HD)
        for number, target in enumerate((key_ref, value_ref)):
            copies.append(pltpu.make_async_copy(in_ref.at[head, number], target.at[0, :, lanes], sem))
    for copy in copies:
        copy.start()
    for copy in copies:
        copy.wait()


def unpack(arrived):
    out = pltpu.HBM((1, PAIR, HEADS * HD), BF16)
    return pl.pallas_call(
        unpack_kernel,
        in_specs=[pl.BlockSpec(memory_space=pltpu.VMEM)],
        out_specs=[pl.BlockSpec(memory_space=pl.ANY)] * 2,
        out_shape=[out, out],
        scratch_shapes=[pltpu.SemaphoreType.DMA],
        name="unpack",
        compiler_params=pltpu.CompilerParams(vmem_limit_bytes=SMALL),
    )(arrived)


def swap(array):
    return lax.all_to_all(array, "g", 0, 0)


def sum_over(lines, axis, steps):
    count = lax.axis_size(axis)
    total = lines
    for step in steps:
        total = total + lax.ppermute(lines, axis, [(source, source ^ step) for source in range(count)])
    return total


def on_device(blocks, q_raw, k_raw, values, d_out, q_gain, k_gain):
    block = lax.axis_index("x")
    member = lax.axis_index("g")
    flags = jnp.stack([block > 0, block < blocks - 1, member < HEADS]).astype(jnp.int32)
    up = [(source, source + 1) for source in range(blocks - 1)]
    down = [(source + 1, source) for source in range(blocks - 1)]
    q_line = q_gain.reshape(1, HD)
    k_line = k_gain.reshape(1, HD)
    gains = jnp.concatenate([q_line, k_line, jnp.ones((6, HD), F32)], axis=0)

    kv = swap(pack(k_raw, values))
    low = lax.ppermute(kv[HALF:], "x", up)
    high = lax.ppermute(kv[:HALF], "x", down)
    qd = swap(pack(q_raw, d_out))
    dq, to_low, to_high, *stored = attention(flags, kv, low, high, qd, gains)
    arrived = swap(dq)
    from_low = lax.ppermute(to_high, "x", up)
    from_high = lax.ppermute(to_low, "x", down)
    own = own_sums(kv, *stored, k_line)
    q_grad, lines = unpack_query(arrived)
    grads = finish(0, kv, own, from_low, k_line)
    grads = finish(1, kv, own, from_high, k_line, grads).reshape(GROUP, 2, PAIR, HD)
    k_grad, v_grad = unpack(swap(grads))
    lines = sum_over(lines, "dp", (1, 2, 3))
    lines = sum_over(lines, "x", (1, 2, 3))
    return (q_grad, k_grad, v_grad, lines[0], lines[1])


def solution(mesh):
    videos, seq = mesh.devices.shape
    blocks = seq // GROUP
    split = Mesh(mesh.devices.reshape(videos, blocks, GROUP), ("dp", "x", "g"))
    tokens = P("dp", ("x", "g"), None)
    return jax.shard_map(
        functools.partial(on_device, blocks),
        mesh=split,
        in_specs=(tokens, tokens, tokens, tokens, P(), P()),
        out_specs=(tokens, tokens, tokens, P(), P()),
        check_vma=False,
    )
```
